128 devices in a mesh: ctx: 16 (over x, z_lo, core), dp: 8 (over z_hi, y).
Axes of the slice: x: 4, y: 4, z: 4 (z_hi: 2, z_lo: 2; z = z_hi * 2 + z_lo), core: 2. Of those that a mesh axis runs over, the one named last changes fastest.
Arguments:
- queries: bfloat16 [8, 2048, 2048], P('dp', 'ctx'), may hold values from -24 to 24
- key_states: bfloat16 [8, 2048, 2048], P('dp', 'ctx'), may hold values from -24 to 24
- value_states: bfloat16 [8, 2048, 2048], P('dp', 'ctx'), may hold values from -6 to 6
- out_grad: bfloat16 [8, 2048, 2048], P('dp', 'ctx'), may hold values from -1.5 to 1.5
- w_out: bfloat16 [2048, 2048], replicated, may hold values from -0.125 to 0.125
- doc_lengths: int32 [8, 8], P('dp'), may hold values from 1 to 1536, 2048 in all within a row
Outputs:
- layer_out: bfloat16 [8, 2048, 2048], P('dp', 'ctx')
- query_grad: bfloat16 [8, 2048, 2048], P('dp', 'ctx')
- key_grad: bfloat16 [8, 2048, 2048], P('dp', 'ctx')
- value_grad: bfloat16 [8, 2048, 2048], P('dp', 'ctx')
- weight_grad: float32 [2048, 2048], P('ctx')
The draws below stay inside these ranges and needn't reach their ends.
Inputs may be any that keep to these rules, and one draw needn't show every extreme that they name: `doc_lengths`: row s lists in order the lengths of the documents packed into sequence s; they sum to 2048, and the longest is exactly 1536.
All inputs are finite; a program needn't handle non-finite values.
Results may differ from the reference program's by a relative error of at most 0.025.
Values may be sent and summed in bfloat16 or wider, within the bound.
A program may use at most 128 MiB of HBM per device.

```python
import math
import jax
import jax.numpy as jnp
import numpy as np
from jax import lax

D = 2048
ATTENTION_HEADS = 16
HEAD_DIM = 128
TOK_DEV = 128
NDOC = 8
GROUP_RATE = 4
FAR_RATE = 16
SEQS = 8
LENGTH = 2048
N_CTX = 16


def draw_queries(key, part):
    own_key = jax.random.fold_in(key, 11)
    result = jnp.clip(jax.random.normal(own_key, (SEQS, LENGTH, D), jnp.float32), -6.0, 6.0)
    return result.astype(jnp.bfloat16)


def draw_key_states(key, part):
    own_key = jax.random.fold_in(key, 12)
    result = jnp.clip(jax.random.normal(own_key, (SEQS, LENGTH, D), jnp.float32), -6.0, 6.0)
    return result.astype(jnp.bfloat16)


def level_of(key, extent, pieces, least, largest):
    def one(axis_at, parts):
        draws = jax.random.uniform(jax.random.fold_in(jax.random.fold_in(key, 6), axis_at), (parts,), jnp.float32, least / len(pieces), largest / len(pieces))
        return jnp.repeat(jnp.exp(draws), extent[axis_at] // parts).reshape((-1,) + (1,) * (len(extent) - axis_at - 1))

    level = one(*pieces[0])
    for cut in pieces[1:]:
        level = level * one(*cut)
    return level


def split_up(count, total, limit, skew):
    portions = [(1 << 20) // math.isqrt(rank ** skew) + 1 for rank in range(2, count + 1)]
    spare, given = total - limit - (count - 1), [1] * (count - 1)
    while spare > 0:
        movable = [i for i in range(count - 1) if given[i] < limit]
        pool, left = sum([portions[i] for i in movable]), spare
        for i in movable:
            extra = min(limit - given[i], max(1, left * portions[i] // pool), spare)
            given[i] = given[i] + extra
            spare = spare - extra
    return np.array([limit] + given)


def uneven(key, amount, total, most, slope):
    if amount == 2:
        one = jax.random.randint(key, (), max(1, total - most), min(most, total - 1) + 1)
        return jnp.stack([one, total - one])
    lengths = jnp.asarray(split_up(amount, total, most, slope), jnp.int32)
    pairs = (amount - 1) // 2
    donor, receiver = lengths[1:1 + 2 * pairs:2], lengths[2:2 + 2 * pairs:2]
    margin = jnp.minimum(donor - 1, most - receiver)
    passed = jax.random.randint(jax.random.fold_in(key, 1), (pairs,), 0, 1 << 20) % (margin + 1)
    lengths = lengths.at[1:1 + 2 * pairs:2].set(donor - passed).at[2:2 + 2 * pairs:2].set(receiver + passed)
    return lengths[jax.random.permutation(jax.random.fold_in(key, 2), amount)]


def noise(key, shape, scale, most, pieces=(), dtype=jnp.bfloat16):
    entries = scale * jax.random.normal(key, shape, jnp.float32)
    if pieces:
        entries = entries * level_of(key, shape, pieces, -0.22, 0.18)
    return jnp.clip(entries, -most, most).astype(dtype)


def setup_inputs(seed: int = 0) -> dict:
    keys = jax.random.split(jax.random.key(seed), 7)
    queries = draw_queries(jax.random.fold_in(keys[6], 71), 0)
    key_states = draw_key_states(jax.random.fold_in(keys[6], 71), 0)
    value_states = noise(keys[2], (SEQS, LENGTH, D), 1.0, 6.0, ((0, 8), (1, 16)))
    out_grad = noise(keys[3], (SEQS, LENGTH, D), 0.25, 1.5, ((0, 8), (1, 16)))
    w_out = noise(keys[4], (D, D), D ** -0.5, 0.125)
    doc_lengths = jax.vmap(lambda own: uneven(own, NDOC, LENGTH, 3 * LENGTH // 4, 2))(jax.random.split(keys[5], SEQS)).reshape((SEQS, NDOC)).astype(jnp.int32)
    return dict(queries=queries, key_states=key_states, value_states=value_states, out_grad=out_grad, w_out=w_out, doc_lengths=doc_lengths)


def branch_lookup(dilation_rate, segment_length):
    seg_count = LENGTH // segment_length
    tokens_per_segment = segment_length // dilation_rate
    segment_number = jnp.arange(seg_count)[:, None, None]
    head_numbers = jnp.arange(ATTENTION_HEADS)[None, :, None]
    is_within_range = jnp.arange(tokens_per_segment)[None, None, :]
    return segment_number * segment_length + is_within_range * dilation_rate + head_numbers % dilation_rate


def one_sequence(bundle, w_out):
    query_seq, key_seq, value_seq, grad_seq, doc_len = bundle
    doc_ends = jnp.cumsum(doc_len)
    doc_of = jnp.sum((jnp.arange(LENGTH)[:, None] >= doc_ends[None, :]).astype(jnp.int32), axis=1)
    query_heads = query_seq.reshape(LENGTH, ATTENTION_HEADS, HEAD_DIM)
    key_heads = key_seq.reshape(LENGTH, ATTENTION_HEADS, HEAD_DIM)
    value_heads = value_seq.reshape(LENGTH, ATTENTION_HEADS, HEAD_DIM)
    head_col = jnp.arange(ATTENTION_HEADS)[None, :, None]
    scale = HEAD_DIM ** -0.5
    branch_settings = ((1, TOK_DEV), (GROUP_RATE, GROUP_RATE * TOK_DEV), (FAR_RATE, LENGTH))
    saved = []
    partial_logs = []
    for dilation_rate, segment_length in branch_settings:
        lookup_table = branch_lookup(dilation_rate, segment_length)
        picked_q = query_heads[lookup_table, head_col].astype(jnp.float32)
        picked_k = key_heads[lookup_table, head_col].astype(jnp.float32)
        picked_v = value_heads[lookup_table, head_col].astype(jnp.float32)
        docs = doc_of[lookup_table]
        order = jnp.arange(lookup_table.shape[2])
        causal = (order[None, :] <= order[:, None])[None, None]
        permitted_mask = causal & (docs[..., :, None] == docs[..., None, :])
        score_matrix = jnp.where(permitted_mask, jnp.einsum("shqe,shke->shqk", picked_q, picked_k) * scale, -jnp.inf)
        part_log = jax.nn.logsumexp(score_matrix, axis=-1)
        full_log = jnp.full((LENGTH, ATTENTION_HEADS), -jnp.inf, jnp.float32).at[lookup_table, head_col].set(part_log)
        partial_logs.append(full_log)
        saved.append((lookup_table, picked_q, picked_k, picked_v, score_matrix))
    total_log_norm = jax.nn.logsumexp(jnp.stack(partial_logs), axis=0)
    mixed_sum = jnp.zeros((LENGTH, ATTENTION_HEADS, HEAD_DIM), jnp.float32)
    probs_saved = []
    for lookup_table, picked_q, picked_k, picked_v, score_matrix in saved:
        softmax_probabilities = jnp.exp(score_matrix - total_log_norm[lookup_table, head_col][..., None])
        weight_matrices = lax.optimization_barrier(softmax_probabilities.astype(jnp.bfloat16)).astype(jnp.float32)
        mixed_sum = mixed_sum.at[lookup_table, head_col].add(jnp.einsum("shqk,shke->shqe", weight_matrices, picked_v))
        probs_saved.append((softmax_probabilities, weight_matrices))
    mixed = mixed_sum.astype(jnp.bfloat16).reshape(LENGTH, D)
    layer_out = jnp.dot(mixed, w_out, preferred_element_type=jnp.float32).astype(jnp.bfloat16)
    blended_gradient = jnp.dot(grad_seq, w_out.T, preferred_element_type=jnp.float32).astype(jnp.bfloat16)
    grad_heads = blended_gradient.reshape(LENGTH, ATTENTION_HEADS, HEAD_DIM).astype(jnp.float32)
    delta_row_values = jnp.sum(grad_heads * mixed.reshape(LENGTH, ATTENTION_HEADS, HEAD_DIM).astype(jnp.float32), axis=-1)
    query_sum = jnp.zeros((LENGTH, ATTENTION_HEADS, HEAD_DIM), jnp.float32)
    key_accumulated = jnp.zeros((LENGTH, ATTENTION_HEADS, HEAD_DIM), jnp.float32)
    value_accumulated = jnp.zeros((LENGTH, ATTENTION_HEADS, HEAD_DIM), jnp.float32)
    for token_position in range(3):
        lookup_table, picked_q, picked_k, picked_v, score_matrix = saved[token_position]
        softmax_probabilities, weight_matrices = probs_saved[token_position]
        picked_g = grad_heads[lookup_table, head_col]
        dprobs = jnp.einsum("shqe,shke->shqk", picked_g, picked_v)
        dscores = softmax_probabilities * (dprobs - delta_row_values[lookup_table, head_col][..., None])
        dscores = lax.optimization_barrier(dscores.astype(jnp.bfloat16)).astype(jnp.float32)
        value_accumulated = value_accumulated.at[lookup_table, head_col].add(jnp.einsum("shqk,shqe->shke", weight_matrices, picked_g))
        key_accumulated = key_accumulated.at[lookup_table, head_col].add(jnp.einsum("shqk,shqe->shke", dscores, picked_q) * scale)
        query_sum = query_sum.at[lookup_table, head_col].add(jnp.einsum("shqk,shke->shqe", dscores, picked_k) * scale)
    blocks_mixed = mixed.reshape(N_CTX, TOK_DEV, D)
    blocks_grad = grad_seq.reshape(N_CTX, TOK_DEV, D)

    def add_block(carry, pair):
        term = lax.dot_general(pair[0], pair[1], (((0,), (0,)), ((), ())), preferred_element_type=jnp.float32)
        return carry + lax.optimization_barrier(term.astype(jnp.bfloat16)).astype(jnp.float32), None

    weight_seq, _ = lax.scan(add_block, jnp.zeros((D, D), jnp.float32), (blocks_mixed, blocks_grad))
    return (layer_out,
            query_sum.astype(jnp.bfloat16).reshape(LENGTH, D),
            key_accumulated.astype(jnp.bfloat16).reshape(LENGTH, D),
            value_accumulated.astype(jnp.bfloat16).reshape(LENGTH, D),
            weight_seq)


def reference(queries, key_states, value_states, out_grad, w_out, doc_lengths):
    def run_one(bundle):
        return one_sequence(bundle, w_out)

    results = lax.map(run_one, (queries, key_states, value_states, out_grad, doc_lengths))
    return results[0], results[1], results[2], results[3], jnp.sum(results[4], axis=0)
```

```python
import functools

import jax
import jax.numpy as jnp
from jax import lax
from jax.experimental import pallas as pl
from jax.experimental.pallas import tpu as pltpu
from jax.sharding import PartitionSpec as P

MESH = pl.DeviceIdType.MESH
BF, F32 = jnp.bfloat16, jnp.float32
HD = 128
SCALE = HD**-0.5
LOG2E = 1.4426950408889634
HIDE = -1e30
WIDTH = 2048
HALF = 1024
GATHERS = (("x", 0, HALF), ("y", HALF, HALF))


def nn(a, b):
    return lax.dot_general(a, b, (((1,), (0,)), ((), ())), preferred_element_type=F32)


def nt(a, b):
    return lax.dot_general(a, b, (((1,), (1,)), ((), ())), preferred_element_type=F32)


def tn(a, b):
    return lax.dot_general(a, b, (((0,), (0,)), ((), ())), preferred_element_type=F32)


def times(n, step):
    return pl.ds(pl.multiple_of(n, step), step)


def kernel(
    docs,
    q_hbm,
    k_hbm,
    v_hbm,
    og_hbm,
    w_hbm,
    lo_out,
    dq_out,
    dk_out,
    dv_out,
    wg_out,
    qkv,
    kvb,
    og_x,
    og_y,
    wo,
    mg,
    mixc,
    mx_x,
    mx_y,
    mx,
    probs,
    bias_l,
    bias_m,
    bias_f,
    sel,
    dkv,
    dqb,
    sb,
    rm,
    rfx,
    fs,
    rfz,
    far_sum,
    spread,
    outs,
    lob,
    t_x,
    t_y,
    r1_x,
    r1_y,
    s2_x,
    s2_y,
    r2_x,
    r2_y,
    s3_x,
    s3_y,
    wgr,
    wgf,
    send_sem,
    recv_sem,
    local_sem,
    last_send,
    last_recv,
):
    c, d = lax.axis_index("ctx"), lax.axis_index("dp")
    x, zl, j = lax.div(c, 4), lax.rem(lax.div(c, 2), 2), lax.rem(c, 2)
    zh, y = lax.div(d, 4), lax.rem(d, 4)
    z = zh * 2 + zl
    og_g, mx_g, t_g = (og_x, og_y), (mx_x, mx_y), (t_x, t_y)
    r1_g, s2_g, r2_g, s3_g = (r1_x, r1_y), (s2_x, s2_y), (r2_x, r2_y), (s3_x, s3_y)

    def at(x_=None, zl_=None, j_=None, zh_=None, y_=None):
        cx = (x if x_ is None else x_) * 4 + (zl if zl_ is None else zl_) * 2 + (j if j_ is None else j_)
        return (cx, (zh if zh_ is None else zh_) * 4 + (y if y_ is None else y_))

    def x_peer(k):
        return at(x_=lax.rem(x + k, 4))

    def y_peer(k):
        return at(y_=lax.rem(y + k, 4))

    def z_peer(k):
        other = lax.rem(z + k, 4)
        return at(zl_=lax.rem(other, 2), zh_=lax.div(other, 2))

    partner, neighbour = at(j_=1 - j), at(zl_=1 - zl)
    counts = [0, 0]

    def send(src, dst, device):
        n = counts[0]
        counts[0] += 1
        copy = pltpu.make_async_remote_copy(
            src_ref=src,
            dst_ref=dst,
            send_sem=send_sem.at[n],
            recv_sem=recv_sem.at[n],
            device_id=device,
            device_id_type=MESH,
        )
        copy.start()
        return copy

    def local(src, dst):
        n = counts[1]
        counts[1] += 1
        copy = pltpu.make_async_copy(src, dst, local_sem.at[n])
        copy.start()
        return copy

    sent, kept = [], []
    own = times(j * 128, 128)
    theirs = times((1 - j) * 128, 128)

    def mine(b):
        return times(256 * (2 * b + j), 256)

    def not_mine(b):
        return times(256 * (2 * b + 1 - j), 256)

    def block(b):
        return pl.ds(256 * b, 256)

    in_kv = [
        local(hbm.at[:, mine(b)], qkv.at[i, own, block(b)])
        for i, hbm in ((1, k_hbm), (2, v_hbm))
        for b in range(4)
    ]
    in_og = [
        local(og_hbm.at[:, pl.ds(c0, nc)], og_g[g].at[a, own])
        for g, (a, (_, c0, nc)) in enumerate(zip((x, y), GATHERS))
    ]
    in_w = [local(w_hbm.at[mine(b)], wo.at[mine(b)]) for b in range(4)]
    in_q = [local(q_hbm.at[:, mine(b)], qkv.at[0, own, block(b)]) for b in range(4)]
    in_w2 = [local(w_hbm.at[not_mine(b)], wo.at[not_mine(b)]) for b in range(4)]

    barrier = pltpu.get_barrier_semaphore()
    near = [partner] + [peer(k) for peer in (x_peer, y_peer, z_peer) for k in (1, 2, 3)]
    for device in near:
        pl.semaphore_signal(barrier, inc=1, device_id=device, device_id_type=MESH)
    for n in range(8):
        a_o, z_ = 2 * j + n // 4, n % 4
        from_x = at(zl_=z_ % 2, j_=zl, zh_=z_ // 2, y_=a_o)
        from_y = at(x_=a_o, zl_=z_ % 2, j_=zl, zh_=z_ // 2, y_=x)
        for cc, dd in (from_x, from_y):

            @pl.when(jnp.logical_or(cc != c, dd != d))
            def _(cc=cc, dd=dd):
                pl.semaphore_signal(barrier, inc=1, device_id=(cc, dd), device_id_type=MESH)

    owner_x = x * 4 + j * 2 + lax.div(y, 2)
    owner_y = y * 4 + j * 2 + lax.div(x, 2)
    away = 16 - (owner_x == c).astype(jnp.int32) - (owner_y == c).astype(jnp.int32)
    pl.semaphore_wait(barrier, len(near) + away)

    swap_kv = [
        send(hbm.at[:, not_mine(b)], qkv.at[i, own, block(b)], partner)
        for i, hbm in ((1, k_hbm), (2, v_hbm))
        for b in range(4)
    ]
    swap_og = [
        send(og_hbm.at[:, pl.ds(c0, nc)], og_g[g].at[a, own], partner)
        for g, (a, (_, c0, nc)) in enumerate(zip((x, y), GATHERS))
    ]
    swap_q = [send(q_hbm.at[:, not_mine(b)], qkv.at[0, own, block(b)], partner) for b in range(4)]
    _, cy, ny = GATHERS[1]
    gather_y = [
        send(og_hbm.at[:, pl.ds(cy, ny)], og_y.at[y, own], y_peer(k)) for k in (1, 2, 3)
    ]

    row = lax.broadcasted_iota(jnp.int32, (256, 256), 0)
    col = lax.broadcasted_iota(jnp.int32, (256, 256), 1)
    far_head = lax.shift_right_logical(row - 128, 4)
    mid_row = 4 * (row & 63) + 2 * j + (lax.shift_right_logical(row, 6) & 1)
    far_row = 16 * (row & 15) + 4 * lax.shift_right_logical(far_head, 1) + 2 * j + (far_head & 1)
    sel[...] = (col == jnp.where(row < 128, mid_row, far_row)).astype(F32).astype(BF)

    far_own = pl.ds(pl.multiple_of(128 + 16 * (2 * x + zl), 16), 16)
    far_near = pl.ds(pl.multiple_of(128 + 16 * (2 * x + 1 - zl), 16), 16)
    mid_own = times(64 * zl, 64)
    for i in (0, 1):
        for copy in in_kv[4 * i : 4 * i + 4]:
            copy.wait()
        for copy in swap_kv[4 * i : 4 * i + 4]:
            copy.wait_recv()
        picked = nn(sel[...], qkv[1 + i]).astype(BF)
        for hh in range(8):
            hc = slice(HD * hh, HD * hh + HD)
            e = hh % 2
            kvb[i, mid_own, hc] = picked[64 * e : 64 * e + 64, hc]
            kvb[i, far_own, hc] = picked[128 + 16 * hh : 144 + 16 * hh, hc]
    far_z = send(kvb.at[:, far_own], kvb.at[:, far_own], neighbour)
    far_x = [send(kvb.at[:, far_own], kvb.at[:, far_own], x_peer(k)) for k in (1, 2, 3)]
    mid_z = send(kvb.at[:, mid_own], kvb.at[:, mid_own], neighbour)

    base = x * 512 + zl * 256
    here = lax.broadcasted_iota(jnp.int32, (256, 128), 0)
    key = lax.broadcasted_iota(jnp.int32, (256, 128), 1)
    pos = base + here
    start = jnp.zeros((256, 128), jnp.int32)
    end = jnp.int32(0)
    for n in range(8):
        end = end + docs[0, n]
        start = jnp.where(pos >= end, end, start)

    def shown(key_pos, extra):
        seen = jnp.logical_and(key_pos <= pos, key_pos >= start)
        if extra is not None:
            seen = jnp.logical_and(seen, extra)
        return jnp.where(seen, 0.0, HIDE).astype(F32)

    bias_l[...] = shown(base + (here & 128) + key, None)
    for e in range(2):
        r = 2 * j + e
        bias_m[e] = shown(x * 512 + 4 * key + r, (here & 3) == r)
    for hh in range(8):
        h = 4 * (hh // 2) + 2 * j + hh % 2
        bias_f[hh] = shown(16 * key + h, (here & 15) == h)

    for copy in in_og:
        copy.wait()
    for copy in swap_og:
        copy.wait_recv()

    def mixed_grad_block(b):
        in_w[b].wait()
        part = nt(og_x[x], wo[mine(b), :HALF]) + nt(og_y[y], wo[mine(b), HALF:])
        mg[:, 256 * b : 256 * b + 256] = part.astype(BF)

    mixed_grad_block(0)
    far_z.wait_recv()
    far_fwd = [send(kvb.at[:, far_near], kvb.at[:, far_near], x_peer(k)) for k in (1, 2, 3)]
    _, cx, nx = GATHERS[0]
    gather_x = [
        send(og_hbm.at[:, pl.ds(cx, nx)], og_x.at[x, own], x_peer(k)) for k in (1, 2, 3)
    ]
    for b in (1, 2, 3):
        mixed_grad_block(b)
    for copy in in_q:
        copy.wait()
    for copy in swap_q + far_x + far_fwd + [mid_z]:
        copy.wait_recv()

    def forward(hh, carry):
        hc = times(hh * HD, HD)
        kb, vb = kvb[0, :, hc], kvb[1, :, hc]
        e = lax.rem(hh, 2)
        for u in range(2):
            ru = slice(128 * u, 128 * u + 128)
            q = qkv[0, ru, hc]
            s_l = nt(q, qkv[1, ru, hc]) * (SCALE * LOG2E) + bias_l[ru]
            s_b = nt(q, kb) * (SCALE * LOG2E)
            s_m = s_b[:, :128] + bias_m[e, ru]
            s_f = s_b[:, 128:] + bias_f[hh, ru]
            top = jnp.max(jnp.maximum(jnp.maximum(s_l, s_m), s_f), axis=1, keepdims=True)
            e_l, e_m, e_f = jnp.exp2(s_l - top), jnp.exp2(s_m - top), jnp.exp2(s_f - top)
            inv = 1.0 / jnp.sum(e_l + e_m + e_f, axis=1, keepdims=True)
            p_l = (e_l * inv).astype(BF)
            p_b = jnp.concatenate([(e_m * inv).astype(BF), (e_f * inv).astype(BF)], axis=1)
            probs[hh, ru, :128] = p_l
            probs[hh, ru, 128:] = p_b
            mixc[ru, hc] = (nn(p_l, qkv[2, ru, hc]) + nn(p_b, vb)).astype(BF)
        return carry

    lax.fori_loop(0, 8, forward, 0)

    mix_sent = []
    for g, (a, peer) in enumerate(((x, x_peer), (y, y_peer))):
        mx_g[g][a] = mixc[:, times(256 * a, 256)]
        mix_sent.append(
            [
                send(mixc.at[:, times(256 * lax.rem(a + k, 4), 256)], mx_g[g].at[a], peer(k))
                for k in (1, 2, 3)
            ]
        )
    swap_mx = [
        send(mixc.at[theirs, block(b)], mx.at[:, mine(b)], partner) for b in range(4)
    ]
    for b in range(4):
        mx[:, mine(b)] = mixc[own, 256 * b : 256 * b + 256]

    def backward(hh, carry):
        hc = times(hh * HD, HD)
        kb, vb = kvb[0, :, hc], kvb[1, :, hc]
        ds_rows = []
        for u in range(2):
            ru = slice(128 * u, 128 * u + 128)
            q, k, v = qkv[0, ru, hc], qkv[1, ru, hc], qkv[2, ru, hc]
            gr = mg[ru, hc]
            delta = jnp.sum(gr.astype(F32) * mixc[ru, hc].astype(F32), axis=1, keepdims=True)
            p_l, p_b = probs[hh, ru, :128], probs[hh, ru, 128:]
            ds_l = (p_l.astype(F32) * (nt(gr, v) - delta)).astype(BF)
            ds_b = (p_b.astype(F32) * (nt(gr, vb) - delta)).astype(BF)
            dqb[ru, hc] = ((nn(ds_l, k) + nn(ds_b, kb)) * SCALE).astype(BF)
            dkv[0, ru, hc] = tn(ds_l, q)
            dkv[1, ru, hc] = tn(p_l, gr)
            ds_rows.append(ds_b)
        sb[0, :, hc] = tn(jnp.concatenate(ds_rows, axis=0), qkv[0, :, hc]).astype(BF)
        sb[1, :, hc] = tn(probs[hh, :, 128:], mg[:, hc]).astype(BF)
        return carry

    lax.fori_loop(0, 8, backward, 0)

    mid_back = send(sb.at[:, times(64 * (1 - zl), 64)], rm, neighbour)
    far_back = [
        send(sb.at[:, pl.ds(pl.multiple_of(128 + 32 * lax.rem(x + k, 4), 32), 32)], rfx.at[k - 1], x_peer(k))
        for k in (1, 2, 3)
    ]

    def give(buf, out):
        for b in range(4):
            kept.append(local(buf.at[own, block(b)], out.at[:, mine(b)]))
            sent.append(send(buf.at[theirs, block(b)], out.at[:, mine(b)], partner))

    give(dqb, dq_out)

    forwarded = []
    for g, (a, copies) in enumerate(((x, gather_x), (y, gather_y))):
        for k, copy in zip((1, 2, 3), copies):
            copy.wait_recv()
            ref = og_g[g].at[lax.rem(a + 4 - k, 4), own]
            forwarded.append(send(ref, ref, partner))

    for copy in in_w2:
        copy.wait()
    for copy in swap_mx:
        copy.wait_recv()

    def out_block(n, carry):
        cols = times(n * 512, 512)
        lob[:, cols] = nn(mx[...], wo[:, cols]).astype(BF)
        return carry

    lax.fori_loop(0, 4, out_block, 0)
    kept.append(local(lob, lo_out))

    for copy in forwarded:
        copy.wait_recv()
    sent_1 = []
    for g, (a_o, peer) in enumerate(((y, y_peer), (x, x_peer))):
        for copy in mix_sent[g]:
            copy.wait_recv()
        turned = mx_g[g][...].reshape(HALF, 256).T

        def tile(n, carry, g=g, turned=turned):
            cols = times(n * 256, 256)
            t_g[g][:, cols] = nn(turned, og_g[g][:, :, cols].reshape(HALF, 256)).astype(BF)
            return carry

        lax.fori_loop(0, GATHERS[g][2] // 256, tile, 0)
        sent_1.append(
            [
                send(t_g[g].at[times(64 * lax.rem(a_o + k, 4), 64)], r1_g[g].at[k - 1], peer(k))
                for k in (1, 2, 3)
            ]
        )

    for copy in far_back:
        copy.wait_recv()
    far_sum[...] = sb[:, pl.ds(pl.multiple_of(128 + 32 * x, 32), 32)].astype(F32)
    for k in range(3):
        far_sum[...] += rfx[k].astype(F32)
    fs[...] = far_sum[:, times(16 * (1 - zl), 16)].astype(BF)
    far_last = send(fs, rfz, neighbour)

    sent_2 = []
    for g, (a_o, _) in enumerate(((y, y_peer), (x, x_peer))):
        for copy in sent_1[g]:
            copy.wait_recv()
        total = t_g[g][times(64 * a_o, 64)].astype(F32)
        for k in range(3):
            total = total + r1_g[g][k].astype(F32)
        s2_g[g][...] = total.astype(BF)
        sent_2.append(
            [
                send(s2_g[g].at[times(16 * lax.rem(z + k, 4), 16)], r2_g[g].at[k - 1], z_peer(k))
                for k in (1, 2, 3)
            ]
        )

    mid_back.wait_recv()
    far_last.wait_recv()
    far_mine = times(16 * zl, 16)
    for i, out in ((0, dk_out), (1, dv_out)):
        spread[...] = jnp.zeros_like(spread)
        for hh in range(8):
            hc = slice(HD * hh, HD * hh + HD)
            e = hh % 2
            spread[64 * e : 64 * e + 64, hc] = (
                sb[i, mid_own, hc].astype(F32) + rm[i, :, hc].astype(F32)
            ).astype(BF)
            spread[128 + 16 * hh : 144 + 16 * hh, hc] = (
                far_sum[i, far_mine, hc] + rfz[i, :, hc].astype(F32)
            ).astype(BF)
        total = dkv[i] + tn(sel[...], spread[...])
        outs[i] = (total * SCALE if i == 0 else total).astype(BF)
        give(outs.at[i], out)

    piece = lax.rem(4 * lax.rem(y, 2) + z, 8), lax.rem(4 * lax.rem(x, 2) + z, 8)
    for g, owner in enumerate((owner_x, owner_y)):
        _, c0, nc = GATHERS[g]
        for copy in sent_2[g]:
            copy.wait_recv()
        total = s2_g[g][times(16 * z, 16)].astype(F32)
        for k in range(3):
            total = total + r2_g[g][k].astype(F32)
        s3_g[g][...] = total.astype(BF)
        dst = wgr.at[times(16 * piece[g], 16), pl.ds(c0, nc)]
        for n in range(8):
            here_too = jnp.logical_and(owner == c, d == n)

            @pl.when(here_too)
            def _(g=g, dst=dst):
                pltpu.make_async_copy(s3_g[g], dst, last_recv.at[8 * g + piece[g]]).start()

            @pl.when(jnp.logical_not(here_too))
            def _(g=g, n=n, owner=owner, dst=dst):
                pltpu.make_async_remote_copy(
                    src_ref=s3_g[g],
                    dst_ref=dst,
                    send_sem=last_send.at[8 * g + n],
                    recv_sem=last_recv.at[8 * g + piece[g]],
                    device_id=(owner, jnp.int32(n)),
                    device_id_type=MESH,
                ).start()

    for g, (_, c0, nc) in enumerate(GATHERS):
        for n in range(8):
            ref = wgr.at[pl.ds(16 * n, 16), pl.ds(c0, nc)]
            pltpu.make_async_copy(s3_g[g], ref, last_recv.at[8 * g + n]).wait()
    wgf[...] = wgr[...].astype(F32)
    kept.append(local(wgf, wg_out))

    for g, owner in enumerate((owner_x, owner_y)):
        for n in range(8):

            @pl.when(jnp.logical_not(jnp.logical_and(owner == c, d == n)))
            def _(g=g, n=n):
                pltpu.make_async_copy(s3_g[g], s3_g[g], last_send.at[8 * g + n]).wait()

    for copy in (
        swap_kv
        + swap_og
        + swap_q
        + gather_y
        + gather_x
        + [far_z, mid_z, mid_back, far_last]
        + far_x
        + far_fwd
        + far_back
        + swap_mx
        + forwarded
        + sum(mix_sent + sent_1 + sent_2, [])
        + sent
    ):
        copy.wait_send()
    for copy in sent:
        copy.wait_recv()
    for copy in kept:
        copy.wait()


def shards(queries, key_states, value_states, out_grad, w_out, doc_lengths):
    rows = queries.shape[1]
    hbm = pl.BlockSpec(memory_space=pl.ANY)
    out16 = jax.ShapeDtypeStruct((rows, WIDTH), BF)
    vm = pltpu.VMEM
    outs = pl.pallas_call(
        kernel,
        out_shape=[out16] * 4 + [jax.ShapeDtypeStruct((rows, WIDTH), F32)],
        in_specs=[pl.BlockSpec(memory_space=pltpu.SMEM)] + [hbm] * 5,
        out_specs=[hbm] * 5,
        scratch_shapes=[
            vm((3, 256, HALF), BF),
            vm((2, 256, HALF), BF),
            vm((4, 256, HALF), BF),
            vm((4, 256, HALF), BF),
            vm((WIDTH, WIDTH), BF),
            vm((256, HALF), BF),
            vm((256, HALF), BF),
            vm((4, 256, 256), BF),
            vm((4, 256, 256), BF),
            vm((128, WIDTH), BF),
            vm((8, 256, 384), BF),
            vm((256, 128), F32),
            vm((2, 256, 128), F32),
            vm((8, 256, 128), F32),
            vm((256, 256), BF),
            vm((2, 256, HALF), F32),
            vm((256, HALF), BF),
            vm((2, 256, HALF), BF),
            vm((2, 64, HALF), BF),
            vm((3, 2, 32, HALF), BF),
            vm((2, 16, HALF), BF),
            vm((2, 16, HALF), BF),
            vm((2, 32, HALF), F32),
            vm((256, HALF), BF),
            vm((2, 256, HALF), BF),
            vm((128, WIDTH), BF),
            vm((256, HALF), BF),
            vm((256, HALF), BF),
            vm((3, 64, HALF), BF),
            vm((3, 64, HALF), BF),
            vm((64, HALF), BF),
            vm((64, HALF), BF),
            vm((3, 16, HALF), BF),
            vm((3, 16, HALF), BF),
            vm((16, HALF), BF),
            vm((16, HALF), BF),
            vm((128, WIDTH), BF),
            vm((128, WIDTH), F32),
            pltpu.SemaphoreType.DMA((80,)),
            pltpu.SemaphoreType.DMA((80,)),
            pltpu.SemaphoreType.DMA((40,)),
            pltpu.SemaphoreType.DMA((16,)),
            pltpu.SemaphoreType.DMA((16,)),
        ],
        compiler_params=pltpu.CompilerParams(
            collective_id=0, has_side_effects=True, vmem_limit_bytes=56 << 20
        ),
        name="dilated_attention",
    )(doc_lengths, queries[0], key_states[0], value_states[0], out_grad[0], w_out)
    return tuple(o[None] for o in outs[:4]) + (outs[4],)


def solution(mesh):
    rows = P("dp", "ctx", None)
    return jax.shard_map(
        shards,
        mesh=mesh,
        in_specs=(rows, rows, rows, rows, P(), P("dp", None)),
        out_specs=(rows, rows, rows, rows, P("ctx", None)),
        check_vma=False,
    )
```

```python
import functools

import jax
import jax.numpy as jnp
from jax import lax
from jax.experimental import pallas as pl
from jax.experimental.pallas import tpu as pltpu
from jax.sharding import PartitionSpec as P

MESH = pl.DeviceIdType.MESH
BF, F32 = jnp.bfloat16, jnp.float32
HD = 128
SCALE = HD**-0.5
LOG2E = 1.4426950408889634
HIDE = -1e30
WIDTH = 2048
HALF = 1024
GATHERS = (("x", 0, HALF), ("y", HALF, HALF))
PART = 512
UNITS = [(g, n) for n in range(HALF // PART) for g in range(2)]


def nn(a, b):
    return lax.dot_general(a, b, (((1,), (0,)), ((), ())), preferred_element_type=F32)


def nt(a, b):
    return lax.dot_general(a, b, (((1,), (1,)), ((), ())), preferred_element_type=F32)


def tn(a, b):
    return lax.dot_general(a, b, (((0,), (0,)), ((), ())), preferred_element_type=F32)


def times(n, step):
    return pl.ds(pl.multiple_of(n, step), step)


def kernel(
    docs,
    q_hbm,
    k_hbm,
    v_hbm,
    og_hbm,
    w_hbm,
    lo_out,
    dq_out,
    dk_out,
    dv_out,
    wg_out,
    kv_full,
    mid_rows,
    qkv,
    kvb,
    og_x,
    og_y,
    wo,
    mg,
    mixc,
    mx_x,
    mx_y,
    mx,
    probs,
    bias_l,
    bias_m,
    bias_f,
    sel,
    dkv,
    dqb,
    sb,
    rm,
    rfx,
    fs,
    rfz,
    far_sum,
    spread,
    outs,
    lob,
    t_x,
    t_y,
    r1_x,
    r1_y,
    s2_x,
    s2_y,
    r2_x,
    r2_y,
    s3_x,
    s3_y,
    wgr,
    send_sem,
    recv_sem,
    local_sem,
    last_send,
    last_recv,
):
    c, d = lax.axis_index("ctx"), lax.axis_index("dp")
    x, zl, j = lax.div(c, 4), lax.rem(lax.div(c, 2), 2), lax.rem(c, 2)
    zh, y = lax.div(d, 4), lax.rem(d, 4)
    z = zh * 2 + zl
    og_g, mx_g, t_g = (og_x, og_y), (mx_x, mx_y), (t_x, t_y)
    r1_g, s2_g, r2_g, s3_g = (r1_x, r1_y), (s2_x, s2_y), (r2_x, r2_y), (s3_x, s3_y)

    def at(x_=None, zl_=None, j_=None, zh_=None, y_=None):
        cx = (x if x_ is None else x_) * 4 + (zl if zl_ is None else zl_) * 2 + (j if j_ is None else j_)
        return (cx, (zh if zh_ is None else zh_) * 4 + (y if y_ is None else y_))

    def diagonal_peer(k):
        return at(x_=lax.rem(x + k, 4), y_=lax.rem(y + 4 - k, 4))

    def x_peer(k):
        return at(x_=lax.rem(x + k, 4))

    def y_peer(k):
        return at(y_=lax.rem(y + k, 4))

    def z_peer(k):
        other = lax.rem(z + k, 4)
        return at(zl_=lax.rem(other, 2), zh_=lax.div(other, 2))

    partner, neighbour, across = at(j_=1 - j), at(zl_=1 - zl), at(zl_=1 - zl, j_=1 - j)
    in_flight = []

    class Sent:
        def __init__(self, src, dst, device):
            n = sum(isinstance(copy, Sent) for copy in in_flight)
            in_flight.append(self)
            self.landed = False
            self.copy = pltpu.make_async_remote_copy(
                src_ref=src,
                dst_ref=dst,
                send_sem=send_sem.at[n],
                recv_sem=recv_sem.at[n],
                device_id=device,
                device_id_type=MESH,
            )
            self.copy.start()

        def wait_recv(self):
            if not self.landed:
                self.landed = True
                self.copy.wait_recv()

        def finish(self):
            self.wait_recv()
            self.copy.wait_send()

    class Local:
        def __init__(self, src, dst):
            n = sum(isinstance(copy, Local) for copy in in_flight)
            in_flight.append(self)
            self.done = False
            self.copy = pltpu.make_async_copy(src, dst, local_sem.at[n])
            self.copy.start()

        def wait(self):
            if not self.done:
                self.done = True
                self.copy.wait()

        finish = wait

    def drain():
        for copy in in_flight:
            copy.finish()

    own = times(j * 128, 128)
    theirs = times((1 - j) * 128, 128)

    def mine(b):
        return times(256 * (2 * b + j), 256)

    def not_mine(b):
        return times(256 * (2 * b + 1 - j), 256)

    def block(b):
        return pl.ds(256 * b, 256)

    in_full = [Local(hbm, kv_full.at[i]) for i, hbm in enumerate((k_hbm, v_hbm))]
    in_kv = [
        Local(hbm.at[:, mine(b)], qkv.at[i, own, block(b)])
        for i, hbm in ((1, k_hbm), (2, v_hbm))
        for b in range(4)
    ]
    in_og = [
        Local(og_hbm.at[:, pl.ds(c0, nc)], og_g[g].at[a, own])
        for g, (a, (_, c0, nc)) in enumerate(zip((x, y), GATHERS))
    ]
    in_w = [Local(w_hbm.at[mine(b)], wo.at[mine(b)]) for b in range(4)]
    in_q = [Local(q_hbm.at[:, mine(b)], qkv.at[0, own, block(b)]) for b in range(4)]
    in_w2 = [Local(w_hbm.at[not_mine(b)], wo.at[not_mine(b)]) for b in range(4)]

    row = lax.broadcasted_iota(jnp.int32, (128, 128), 0)
    col = lax.broadcasted_iota(jnp.int32, (128, 128), 1)
    pick = (col == 4 * (row & 31) + lax.shift_right_logical(row, 5)).astype(F32).astype(BF)
    for i in (0, 1):
        in_full[i].wait()
        picked = nn(pick, kv_full[i]).astype(BF)
        for core in (0, 1):
            for hh in range(8):
                h, r = 4 * (hh // 2) + 2 * core + hh % 2, 2 * core + hh % 2
                mid_rows[core, i, :, HD * hh : HD * hh + HD] = picked[32 * r : 32 * r + 32, HD * h : HD * h + HD]

    barrier = pltpu.get_barrier_semaphore()
    near = [partner, across] + [
        peer(k) for peer in (x_peer, y_peer, z_peer, diagonal_peer) for k in (1, 2, 3)
    ]
    for device in near:
        pl.semaphore_signal(barrier, inc=1, device_id=device, device_id_type=MESH)
    for n in range(8):
        a, b = 2 * j + n // 4, n % 4
        from_x = at(zl_=n // 4, j_=zl, zh_=j, y_=b)
        from_y = at(x_=a, zl_=b % 2, j_=zl, zh_=b // 2, y_=lax.rem(x + 4 - a, 4))
        for cc, dd in (from_x, from_y):

            @pl.when(jnp.logical_or(cc != c, dd != d))
            def _(cc=cc, dd=dd):
                pl.semaphore_signal(barrier, inc=1, device_id=(cc, dd), device_id_type=MESH)

    owner_x = x * 4 + j * 2 + zh
    owner_y = lax.rem(x + y, 4) * 4 + j * 2 + lax.div(x, 2)
    away = 16 - (owner_x == c).astype(jnp.int32) - (owner_y == c).astype(jnp.int32)
    pl.semaphore_wait(barrier, len(near) + away)

    mid_here = pl.ds(pl.multiple_of(64 * zl + 32 * j, 32), 32)
    mid_sent = [
        Sent(mid_rows.at[j], kvb.at[:, mid_here], neighbour),
        Sent(mid_rows.at[1 - j], kvb.at[:, mid_here], across),
    ]
    swap_kv = [
        Sent(hbm.at[:, not_mine(b)], qkv.at[i, own, block(b)], partner)
        for i, hbm in ((1, k_hbm), (2, v_hbm))
        for b in range(4)
    ]
    mid_sent.append(Sent(mid_rows.at[1 - j], kvb.at[:, mid_here], partner))
    kvb[:, mid_here] = mid_rows[j]
    swap_og = [
        Sent(og_hbm.at[:, pl.ds(c0, nc)], og_g[g].at[a, own], partner)
        for g, (a, (_, c0, nc)) in enumerate(zip((x, y), GATHERS))
    ]
    swap_q = [Sent(q_hbm.at[:, not_mine(b)], qkv.at[0, own, block(b)], partner) for b in range(4)]
    _, cy, ny = GATHERS[1]
    gather_y = [
        Sent(og_hbm.at[:, pl.ds(cy, ny)], og_y.at[y, own], y_peer(k)) for k in (1, 2, 3)
    ]

    row = lax.broadcasted_iota(jnp.int32, (256, 256), 0)
    col = lax.broadcasted_iota(jnp.int32, (256, 256), 1)
    far_head = lax.shift_right_logical(row - 128, 4)
    mid_row = 4 * (row & 63) + 2 * j + (lax.shift_right_logical(row, 6) & 1)
    far_row = 16 * (row & 15) + 4 * lax.shift_right_logical(far_head, 1) + 2 * j + (far_head & 1)
    sel[...] = (col == jnp.where(row < 128, mid_row, far_row)).astype(F32).astype(BF)

    far_own = pl.ds(pl.multiple_of(128 + 16 * (2 * x + zl), 16), 16)
    far_near = pl.ds(pl.multiple_of(128 + 16 * (2 * x + 1 - zl), 16), 16)
    mid_own = times(64 * zl, 64)
    for i in (0, 1):
        for copy in in_kv[4 * i : 4 * i + 4]:
            copy.wait()
        for copy in swap_kv[4 * i : 4 * i + 4]:
            copy.wait_recv()
        picked = nn(sel[128:], qkv[1 + i]).astype(BF)
        for hh in range(8):
            hc = slice(HD * hh, HD * hh + HD)
            kvb[i, far_own, hc] = picked[16 * hh : 16 * hh + 16, hc]
    far_z = Sent(kvb.at[:, far_own], kvb.at[:, far_own], neighbour)
    far_x = [Sent(kvb.at[:, far_own], kvb.at[:, far_own], x_peer(k)) for k in (1, 2, 3)]

    base = x * 512 + zl * 256
    here = lax.broadcasted_iota(jnp.int32, (256, 128), 0)
    key = lax.broadcasted_iota(jnp.int32, (256, 128), 1)
    pos = base + here
    start = jnp.zeros((256, 128), jnp.int32)
    end = jnp.int32(0)
    for n in range(8):
        end = end + docs[0, n]
        start = jnp.where(pos >= end, end, start)

    def shown(key_pos, extra):
        seen = jnp.logical_and(key_pos <= pos, key_pos >= start)
        if extra is not None:
            seen = jnp.logical_and(seen, extra)
        return jnp.where(seen, 0.0, HIDE).astype(F32)

    bias_l[...] = shown(base + (here & 128) + key, None)
    for e in range(2):
        r = 2 * j + e
        bias_m[e] = shown(x * 512 + 4 * key + r, (here & 3) == r)
    for hh in range(8):
        h = 4 * (hh // 2) + 2 * j + hh % 2
        bias_f[hh] = shown(16 * key + h, (here & 15) == h)

    for copy in in_og:
        copy.wait()
    for copy in swap_og:
        copy.wait_recv()

    def mixed_grad_block(b):
        in_w[b].wait()
        part = nt(og_x[x], wo[mine(b), :HALF]) + nt(og_y[y], wo[mine(b), HALF:])
        mg[:, 256 * b : 256 * b + 256] = part.astype(BF)

    mixed_grad_block(0)
    far_z.wait_recv()
    far_fwd = [Sent(kvb.at[:, far_near], kvb.at[:, far_near], x_peer(k)) for k in (1, 2, 3)]
    _, cx, nx = GATHERS[0]
    gather_x = [
        Sent(og_hbm.at[:, pl.ds(cx, nx)], og_x.at[x, own], x_peer(k)) for k in (1, 2, 3)
    ]
    for b in (1, 2, 3):
        mixed_grad_block(b)
    for copy in in_q:
        copy.wait()
    for copy in swap_q + mid_sent + far_x + far_fwd:
        copy.wait_recv()

    def forward(hh, carry):
        hc = times(hh * HD, HD)
        kb, vb = kvb[0, :, hc], kvb[1, :, hc]
        e = lax.rem(hh, 2)
        for u in range(2):
            ru = slice(128 * u, 128 * u + 128)
            q = qkv[0, ru, hc]
            s_l = nt(q, qkv[1, ru, hc]) * (SCALE * LOG2E) + bias_l[ru]
            s_b = nt(q, kb) * (SCALE * LOG2E)
            s_m = s_b[:, :128] + bias_m[e, ru]
            s_f = s_b[:, 128:] + bias_f[hh, ru]
            top = jnp.max(jnp.maximum(jnp.maximum(s_l, s_m), s_f), axis=1, keepdims=True)
            e_l, e_m, e_f = jnp.exp2(s_l - top), jnp.exp2(s_m - top), jnp.exp2(s_f - top)
            inv = 1.0 / jnp.sum(e_l + e_m + e_f, axis=1, keepdims=True)
            p_l = (e_l * inv).astype(BF)
            p_b = jnp.concatenate([(e_m * inv).astype(BF), (e_f * inv).astype(BF)], axis=1)
            probs[hh, ru, :128] = p_l
            probs[hh, ru, 128:] = p_b
            mixc[ru, hc] = (nn(p_l, qkv[2, ru, hc]) + nn(p_b, vb)).astype(BF)
        return carry

    lax.fori_loop(0, 8, forward, 0, unroll=4)

    mix_sent = []
    for g, (a, peer, first) in enumerate(((x, x_peer, 0), (y, y_peer, x))):
        mx_g[g][a] = mixc[:, times(256 * lax.rem(first + a, 4), 256)]
        mix_sent.append(
            [
                Sent(mixc.at[:, times(256 * lax.rem(first + a + k, 4), 256)], mx_g[g].at[a], peer(k))
                for k in (1, 2, 3)
            ]
        )
    swap_mx = [
        Sent(mixc.at[theirs, block(b)], mx.at[:, mine(b)], partner) for b in range(4)
    ]
    for b in range(4):
        mx[:, mine(b)] = mixc[own, 256 * b : 256 * b + 256]

    forwarded = []
    for g, (a, copies) in enumerate(((x, gather_x), (y, gather_y))):
        for k, copy in zip((1, 2, 3), copies):
            copy.wait_recv()
            ref = og_g[g].at[lax.rem(a + 4 - k, 4), own]
            forwarded.append(Sent(ref, ref, partner))

    def backward(hh, carry):
        hc = times(hh * HD, HD)
        kb, vb = kvb[0, :, hc], kvb[1, :, hc]
        ds_rows = []
        for u in range(2):
            ru = slice(128 * u, 128 * u + 128)
            q, k, v = qkv[0, ru, hc], qkv[1, ru, hc], qkv[2, ru, hc]
            gr = mg[ru, hc]
            delta = jnp.sum(gr.astype(F32) * mixc[ru, hc].astype(F32), axis=1, keepdims=True)
            p_l, p_b = probs[hh, ru, :128], probs[hh, ru, 128:]
            ds_l = (p_l.astype(F32) * (nt(gr, v) - delta)).astype(BF)
            ds_b = (p_b.astype(F32) * (nt(gr, vb) - delta)).astype(BF)
            dqb[ru, hc] = ((nn(ds_l, k) + nn(ds_b, kb)) * SCALE).astype(BF)
            dkv[0, ru, hc] = tn(ds_l, q)
            dkv[1, ru, hc] = tn(p_l, gr)
            ds_rows.append(ds_b)
        sb[0, :, hc] = tn(jnp.concatenate(ds_rows, axis=0), qkv[0, :, hc]).astype(BF)
        sb[1, :, hc] = tn(probs[hh, :, 128:], mg[:, hc]).astype(BF)
        return carry

    lax.fori_loop(0, 8, backward, 0, unroll=4)

    mid_back = Sent(sb.at[:, times(64 * (1 - zl), 64)], rm, neighbour)
    far_back = [
        Sent(sb.at[:, pl.ds(pl.multiple_of(128 + 32 * lax.rem(x + k, 4), 32), 32)], rfx.at[k - 1], x_peer(k))
        for k in (1, 2, 3)
    ]

    def give(buf, out):
        for b in range(4):
            Local(buf.at[own, block(b)], out.at[:, mine(b)])
            Sent(buf.at[theirs, block(b)], out.at[:, mine(b)], partner)

    give(dqb, dq_out)

    for copy in forwarded:
        copy.wait_recv()
    around = (z, z_peer), (x, diagonal_peer)
    turned = []
    for g in range(2):
        for copy in mix_sent[g]:
            copy.wait_recv()
        turned.append(mx_g[g][...].reshape(HALF, 256).T)
    sent_1 = []
    for g, n in UNITS:
        for c0 in range(PART * n, PART * n + PART, 256):
            cols = slice(c0, c0 + 256)
            t_g[g][:, cols] = nn(turned[g], og_g[g][:, :, cols].reshape(HALF, 256)).astype(BF)
        cols = pl.ds(PART * n, PART)
        a, peer = around[g]
        sent_1.append(
            [
                Sent(t_g[g].at[times(64 * lax.rem(a + k, 4), 64), cols], r1_g[g].at[k - 1, :, cols], peer(k))
                for k in (1, 2, 3)
            ]
        )

    for copy in in_w2:
        copy.wait()
    for copy in swap_mx:
        copy.wait_recv()

    def out_block(n, carry):
        cols = times(n * 512, 512)
        lob[:, cols] = nn(mx[...], wo[:, cols]).astype(BF)
        return carry

    lax.fori_loop(0, 4, out_block, 0)
    Local(lob, lo_out)

    for copy in far_back:
        copy.wait_recv()
    far_sum[...] = sb[:, pl.ds(pl.multiple_of(128 + 32 * x, 32), 32)].astype(F32)
    for k in range(3):
        far_sum[...] += rfx[k].astype(F32)
    fs[...] = far_sum[:, times(16 * (1 - zl), 16)].astype(BF)
    far_last = Sent(fs, rfz, neighbour)

    around_2 = (y, y_peer), (z, z_peer)
    sent_2 = []
    for (g, n), copies in zip(UNITS, sent_1):
        for copy in copies:
            copy.wait_recv()
        cols = slice(PART * n, PART * n + PART)
        total = t_g[g][times(64 * around[g][0], 64), cols].astype(F32)
        for k in range(3):
            total = total + r1_g[g][k, :, cols].astype(F32)
        s2_g[g][:, cols] = total.astype(BF)
        cols = pl.ds(PART * n, PART)
        a, peer = around_2[g]
        sent_2.append(
            [
                Sent(s2_g[g].at[times(16 * lax.rem(a + k, 4), 16), cols], r2_g[g].at[k - 1, :, cols], peer(k))
                for k in (1, 2, 3)
            ]
        )

    mid_back.wait_recv()
    far_last.wait_recv()
    far_mine = times(16 * zl, 16)
    for i, out in ((0, dk_out), (1, dv_out)):
        spread[...] = jnp.zeros_like(spread)
        for hh in range(8):
            hc = slice(HD * hh, HD * hh + HD)
            e = hh % 2
            spread[64 * e : 64 * e + 64, hc] = (
                sb[i, mid_own, hc].astype(F32) + rm[i, :, hc].astype(F32)
            ).astype(BF)
            spread[128 + 16 * hh : 144 + 16 * hh, hc] = (
                far_sum[i, far_mine, hc] + rfz[i, :, hc].astype(F32)
            ).astype(BF)
        total = dkv[i] + tn(sel[...], spread[...])
        outs[i] = (total * SCALE if i == 0 else total).astype(BF)
        give(outs.at[i], out)

    piece = lax.rem(4 * zl + y, 8), lax.rem(4 * lax.rem(x, 2) + z, 8)
    owners = owner_x, owner_y
    for m, ((g, n), copies) in enumerate(zip(UNITS, sent_2)):
        for copy in copies:
            copy.wait_recv()
        cols = slice(PART * n, PART * n + PART)
        total = s2_g[g][times(16 * around_2[g][0], 16), cols].astype(F32)
        for k in range(3):
            total = total + r2_g[g][k, :, cols].astype(F32)
        s3_g[g][:, cols] = total.astype(BF)
        src = s3_g[g].at[:, pl.ds(PART * n, PART)]
        dst = wgr.at[times(16 * piece[g], 16), pl.ds(GATHERS[g][1] + PART * n, PART)]
        for dp in range(8):
            stays = jnp.logical_and(owners[g] == c, d == dp)

            @pl.when(stays)
            def _(m=m, g=g, src=src, dst=dst):
                pltpu.make_async_copy(src, dst, last_recv.at[8 * m + piece[g]]).start()

            @pl.when(jnp.logical_not(stays))
            def _(m=m, g=g, dp=dp, src=src, dst=dst):
                pltpu.make_async_remote_copy(
                    src_ref=src,
                    dst_ref=dst,
                    send_sem=last_send.at[8 * m + dp],
                    recv_sem=last_recv.at[8 * m + piece[g]],
                    device_id=(owners[g], jnp.int32(dp)),
                    device_id_type=MESH,
                ).start()

    for m, (g, n) in enumerate(UNITS):
        src = s3_g[g].at[:, pl.ds(PART * n, PART)]
        for k in range(8):
            ref = wgr.at[pl.ds(16 * k, 16), pl.ds(GATHERS[g][1] + PART * n, PART)]
            pltpu.make_async_copy(src, ref, last_recv.at[8 * m + k]).wait()
    Local(wgr, wg_out)

    for m, (g, n) in enumerate(UNITS):
        src = s3_g[g].at[:, pl.ds(PART * n, PART)]
        for dp in range(8):

            @pl.when(jnp.logical_not(jnp.logical_and(owners[g] == c, d == dp)))
            def _(m=m, dp=dp, src=src):
                pltpu.make_async_copy(src, src, last_send.at[8 * m + dp]).wait()

    drain()


def place(lo, dq, dk, dv, wg, lo_out, dq_out, dk_out, dv_out, wg_out, held, wg32, sems):
    pairs = ((wg, None), (lo, lo_out), (dq, dq_out), (dk, dk_out), (dv, dv_out))
    taken = [pltpu.make_async_copy(src, held.at[n], sems.at[n]) for n, (src, _) in enumerate(pairs)]
    for copy in taken:
        copy.start()
    given = []
    for n, (_, dst) in enumerate(pairs):
        taken[n].wait()
        if dst is None:
            wg32[...] = held[n].astype(F32)
        given.append(
            pltpu.make_async_copy(wg32 if dst is None else held.at[n], wg_out if dst is None else dst, sems.at[5 + n])
        )
        given[n].start()
    for copy in given:
        copy.wait()


def shards(queries, key_states, value_states, out_grad, w_out, doc_lengths):
    rows = queries.shape[1]
    hbm = pl.BlockSpec(memory_space=pl.ANY)
    out16 = jax.ShapeDtypeStruct((rows, WIDTH), BF)
    vm = pltpu.VMEM
    outs = pl.pallas_call(
        kernel,
        out_shape=[out16] * 5,
        in_specs=[pl.BlockSpec(memory_space=pltpu.SMEM)] + [hbm] * 5,
        out_specs=[hbm] * 5,
        scratch_shapes=[
            vm((2, 128, WIDTH), BF),
            vm((2, 2, 32, HALF), BF),
            vm((3, 256, HALF), BF),
            vm((2, 256, HALF), BF),
            vm((4, 256, HALF), BF),
            vm((4, 256, HALF), BF),
            vm((WIDTH, WIDTH), BF),
            vm((256, HALF), BF),
            vm((256, HALF), BF),
            vm((4, 256, 256), BF),
            vm((4, 256, 256), BF),
            vm((128, WIDTH), BF),
            vm((8, 256, 384), BF),
            vm((256, 128), F32),
            vm((2, 256, 128), F32),
            vm((8, 256, 128), F32),
            vm((256, 256), BF),
            vm((2, 256, HALF), F32),
            vm((256, HALF), BF),
            vm((2, 256, HALF), BF),
            vm((2, 64, HALF), BF),
            vm((3, 2, 32, HALF), BF),
            vm((2, 16, HALF), BF),
            vm((2, 16, HALF), BF),
            vm((2, 32, HALF), F32),
            vm((256, HALF), BF),
            vm((2, 256, HALF), BF),
            vm((128, WIDTH), BF),
            vm((256, HALF), BF),
            vm((256, HALF), BF),
            vm((3, 64, HALF), BF),
            vm((3, 64, HALF), BF),
            vm((64, HALF), BF),
            vm((64, HALF), BF),
            vm((3, 16, HALF), BF),
            vm((3, 16, HALF), BF),
            vm((16, HALF), BF),
            vm((16, HALF), BF),
            vm((128, WIDTH), BF),
            pltpu.SemaphoreType.DMA((96,)),
            pltpu.SemaphoreType.DMA((96,)),
            pltpu.SemaphoreType.DMA((40,)),
            pltpu.SemaphoreType.DMA((32,)),
            pltpu.SemaphoreType.DMA((32,)),
        ],
        compiler_params=pltpu.CompilerParams(
            collective_id=0, has_side_effects=True, vmem_limit_bytes=56 << 20
        ),
        name="dilated_attention",
    )(doc_lengths, queries[0], key_states[0], value_states[0], out_grad[0], w_out)
    outs = pl.pallas_call(
        place,
        out_shape=[out16] * 4 + [jax.ShapeDtypeStruct((rows, WIDTH), F32)],
        in_specs=[hbm] * 5,
        out_specs=[hbm] * 5,
        scratch_shapes=[vm((5, rows, WIDTH), BF), vm((rows, WIDTH), F32), pltpu.SemaphoreType.DMA((10,))],
        name="place_results",
    )(*outs)
    return tuple(o[None] for o in outs[:4]) + (outs[4],)


def solution(mesh):
    rows = P("dp", "ctx", None)
    return jax.shard_map(
        shards,
        mesh=mesh,
        in_specs=(rows, rows, rows, rows, P(), P("dp", None)),
        out_specs=(rows, rows, rows, rows, P("ctx", None)),
        check_vma=False,
    )
```

```python
import functools

import jax
import jax.numpy as jnp
from jax import lax
from jax.experimental import pallas as pl
from jax.experimental.pallas import tpu as pltpu
from jax.sharding import PartitionSpec as P

MESH = pl.DeviceIdType.MESH
BF, F32 = jnp.bfloat16, jnp.float32
HD = 128
SCALE = HD**-0.5
LOG2E = 1.4426950408889634
HIDE = -1e30
WIDTH = 2048
HALF = 1024
GATHERS = (("x", 0, HALF), ("y", HALF, HALF))
PART = 512
UNITS = [(g, n) for n in range(HALF // PART) for g in range(2)]


def nn(a, b):
    return lax.dot_general(a, b, (((1,), (0,)), ((), ())), preferred_element_type=F32)


def nt(a, b):
    return lax.dot_general(a, b, (((1,), (1,)), ((), ())), preferred_element_type=F32)


def tn(a, b):
    return lax.dot_general(a, b, (((0,), (0,)), ((), ())), preferred_element_type=F32)


def times(n, step):
    return pl.ds(pl.multiple_of(n, step), step)


def kernel(
    docs,
    q_hbm,
    k_hbm,
    v_hbm,
    og_hbm,
    w_hbm,
    lo_out,
    dq_out,
    dk_out,
    dv_out,
    wg_out,
    qkv,
    kvb,
    og_x,
    og_y,
    wo,
    mg,
    mixc,
    mx_x,
    mx_y,
    mx,
    probs,
    bias_l,
    bias_m,
    bias_f,
    sel,
    dkv,
    dqb,
    sb,
    rm,
    rfx,
    fs,
    rfz,
    far_sum,
    spread,
    outs,
    lob,
    t_x,
    t_y,
    r1_x,
    r1_y,
    s2_x,
    s2_y,
    r2_x,
    r2_y,
    s3_x,
    s3_y,
    wgr,
    send_sem,
    recv_sem,
    local_sem,
    last_send,
    last_recv,
):
    c, d = lax.axis_index("ctx"), lax.axis_index("dp")
    x, zl, j = lax.div(c, 4), lax.rem(lax.div(c, 2), 2), lax.rem(c, 2)
    zh, y = lax.div(d, 4), lax.rem(d, 4)
    z = zh * 2 + zl
    og_g, mx_g, t_g = (og_x, og_y), (mx_x, mx_y), (t_x, t_y)
    r1_g, s2_g, r2_g, s3_g = (r1_x, r1_y), (s2_x, s2_y), (r2_x, r2_y), (s3_x, s3_y)

    def at(x_=None, zl_=None, j_=None, zh_=None, y_=None):
        cx = (x if x_ is None else x_) * 4 + (zl if zl_ is None else zl_) * 2 + (j if j_ is None else j_)
        return (cx, (zh if zh_ is None else zh_) * 4 + (y if y_ is None else y_))

    def diagonal_peer(k):
        return at(x_=lax.rem(x + k, 4), y_=lax.rem(y + 4 - k, 4))

    def x_peer(k):
        return at(x_=lax.rem(x + k, 4))

    def y_peer(k):
        return at(y_=lax.rem(y + k, 4))

    def z_peer(k):
        other = lax.rem(z + k, 4)
        return at(zl_=lax.rem(other, 2), zh_=lax.div(other, 2))

    partner, neighbour = at(j_=1 - j), at(zl_=1 - zl)
    in_flight = []

    class Sent:
        def __init__(self, src, dst, device):
            n = sum(isinstance(copy, Sent) for copy in in_flight)
            in_flight.append(self)
            self.landed = False
            self.copy = pltpu.make_async_remote_copy(
                src_ref=src,
                dst_ref=dst,
                send_sem=send_sem.at[n],
                recv_sem=recv_sem.at[n],
                device_id=device,
                device_id_type=MESH,
            )
            self.copy.start()

        def wait_recv(self):
            if not self.landed:
                self.landed = True
                self.copy.wait_recv()

        def finish(self):
            self.wait_recv()
            self.copy.wait_send()

    class Local:
        def __init__(self, src, dst):
            n = sum(isinstance(copy, Local) for copy in in_flight)
            in_flight.append(self)
            self.done = False
            self.copy = pltpu.make_async_copy(src, dst, local_sem.at[n])
            self.copy.start()

        def wait(self):
            if not self.done:
                self.done = True
                self.copy.wait()

        finish = wait

    def drain():
        for copy in in_flight:
            copy.finish()

    own = times(j * 128, 128)
    theirs = times((1 - j) * 128, 128)

    def mine(b):
        return times(256 * (2 * b + j), 256)

    def not_mine(b):
        return times(256 * (2 * b + 1 - j), 256)

    def block(b):
        return pl.ds(256 * b, 256)

    in_kv = [
        Local(hbm.at[:, mine(b)], qkv.at[i, own, block(b)])
        for i, hbm in ((1, k_hbm), (2, v_hbm))
        for b in range(4)
    ]
    in_og = [
        Local(og_hbm.at[:, pl.ds(c0, nc)], og_g[g].at[a, own])
        for g, (a, (_, c0, nc)) in enumerate(zip((x, y), GATHERS))
    ]
    in_w = [Local(w_hbm.at[mine(b)], wo.at[mine(b)]) for b in range(4)]
    in_q = [Local(q_hbm.at[:, mine(b)], qkv.at[0, own, block(b)]) for b in range(4)]
    in_w2 = [Local(w_hbm.at[not_mine(b)], wo.at[not_mine(b)]) for b in range(4)]

    barrier = pltpu.get_barrier_semaphore()
    near = [partner] + [
        peer(k) for peer in (x_peer, y_peer, z_peer, diagonal_peer) for k in (1, 2, 3)
    ]
    for device in near:
        pl.semaphore_signal(barrier, inc=1, device_id=device, device_id_type=MESH)
    for n in range(8):
        a, b = 2 * j + n // 4, n % 4
        from_x = at(zl_=n // 4, j_=zl, zh_=j, y_=b)
        from_y = at(x_=a, zl_=b % 2, j_=zl, zh_=b // 2, y_=lax.rem(x + 4 - a, 4))
        for cc, dd in (from_x, from_y):

            @pl.when(jnp.logical_or(cc != c, dd != d))
            def _(cc=cc, dd=dd):
                pl.semaphore_signal(barrier, inc=1, device_id=(cc, dd), device_id_type=MESH)

    owner_x = x * 4 + j * 2 + zh
    owner_y = lax.rem(x + y, 4) * 4 + j * 2 + lax.div(x, 2)
    away = 16 - (owner_x == c).astype(jnp.int32) - (owner_y == c).astype(jnp.int32)
    pl.semaphore_wait(barrier, len(near) + away)

    swap_kv = [
        Sent(hbm.at[:, not_mine(b)], qkv.at[i, own, block(b)], partner)
        for i, hbm in ((1, k_hbm), (2, v_hbm))
        for b in range(4)
    ]
    swap_og = [
        Sent(og_hbm.at[:, pl.ds(c0, nc)], og_g[g].at[a, own], partner)
        for g, (a, (_, c0, nc)) in enumerate(zip((x, y), GATHERS))
    ]
    swap_q = [Sent(q_hbm.at[:, not_mine(b)], qkv.at[0, own, block(b)], partner) for b in range(4)]

    def gather(g):
        a, peer = ((x, x_peer), (y, y_peer))[g]
        _, c0, nc = GATHERS[g]
        return [Sent(og_hbm.at[:, pl.ds(c0, nc)], og_g[g].at[a, own], peer(k)) for k in (1, 3)]

    def relay(g, copies):
        a, peer = ((x, x_peer), (y, y_peer))[g]
        passed = []
        for n, (k, copy) in enumerate(zip((1, 3), copies)):
            copy.wait_recv()
            ref = og_g[g].at[lax.rem(a + 4 - k, 4), pl.ds(pl.multiple_of(128 * j + 64 * n, 64), 64)]
            passed.append(Sent(ref, ref, peer(k)))
        return passed

    def to_partner(g, k):
        a = (x, y)[g]
        ref = og_g[g].at[lax.rem(a + k, 4), own]
        return Sent(ref, ref, partner)

    gather_y = gather(1)

    row = lax.broadcasted_iota(jnp.int32, (256, 256), 0)
    col = lax.broadcasted_iota(jnp.int32, (256, 256), 1)
    far_head = lax.shift_right_logical(row - 128, 4)
    mid_row = 4 * (row & 63) + 2 * j + (lax.shift_right_logical(row, 6) & 1)
    far_row = 16 * (row & 15) + 4 * lax.shift_right_logical(far_head, 1) + 2 * j + (far_head & 1)
    sel[...] = (col == jnp.where(row < 128, mid_row, far_row)).astype(F32).astype(BF)

    far_own = pl.ds(pl.multiple_of(128 + 16 * (2 * x + zl), 16), 16)
    far_near = pl.ds(pl.multiple_of(128 + 16 * (2 * x + 1 - zl), 16), 16)
    mid_own = times(64 * zl, 64)
    for i in (0, 1):
        for copy in in_kv[4 * i : 4 * i + 4]:
            copy.wait()
        for copy in swap_kv[4 * i : 4 * i + 4]:
            copy.wait_recv()
        picked = nn(sel[...], qkv[1 + i]).astype(BF)
        for hh in range(8):
            hc = slice(HD * hh, HD * hh + HD)
            e = hh % 2
            kvb[i, mid_own, hc] = picked[64 * e : 64 * e + 64, hc]
            kvb[i, far_own, hc] = picked[128 + 16 * hh : 144 + 16 * hh, hc]
    far_z = Sent(kvb.at[:, far_own], kvb.at[:, far_own], neighbour)
    far_x = [Sent(kvb.at[:, far_own], kvb.at[:, far_own], x_peer(k)) for k in (1, 2, 3)]

    mid_sent = [Sent(kvb.at[:, mid_own], kvb.at[:, mid_own], neighbour)]
    base = x * 512 + zl * 256
    here = lax.broadcasted_iota(jnp.int32, (256, 128), 0)
    key = lax.broadcasted_iota(jnp.int32, (256, 128), 1)
    pos = base + here
    start = jnp.zeros((256, 128), jnp.int32)
    end = jnp.int32(0)
    for n in range(8):
        end = end + docs[0, n]
        start = jnp.where(pos >= end, end, start)

    def shown(key_pos, extra):
        seen = jnp.logical_and(key_pos <= pos, key_pos >= start)
        if extra is not None:
            seen = jnp.logical_and(seen, extra)
        return jnp.where(seen, 0.0, HIDE).astype(F32)

    bias_l[...] = shown(base + (here & 128) + key, None)
    for e in range(2):
        r = 2 * j + e
        bias_m[e] = shown(x * 512 + 4 * key + r, (here & 3) == r)
    for hh in range(8):
        h = 4 * (hh // 2) + 2 * j + hh % 2
        bias_f[hh] = shown(16 * key + h, (here & 15) == h)

    for copy in in_og:
        copy.wait()
    for copy in swap_og:
        copy.wait_recv()

    def mixed_grad_block(b):
        in_w[b].wait()
        part = nt(og_x[x], wo[mine(b), :HALF]) + nt(og_y[y], wo[mine(b), HALF:])
        mg[:, 256 * b : 256 * b + 256] = part.astype(BF)

    mixed_grad_block(0)
    far_z.wait_recv()
    far_fwd = [Sent(kvb.at[:, far_near], kvb.at[:, far_near], x_peer(k)) for k in (1, 2, 3)]
    gather_x = gather(0)
    for b in (1, 2, 3):
        mixed_grad_block(b)
    relay_y = relay(1, gather_y)
    forwarded = [to_partner(1, k) for k in (1, 3)]
    for copy in in_q:
        copy.wait()
    for copy in swap_q + mid_sent + far_x + far_fwd:
        copy.wait_recv()

    def forward(hh, carry):
        hc = times(hh * HD, HD)
        kb, vb = kvb[0, :, hc], kvb[1, :, hc]
        e = lax.rem(hh, 2)
        for u in range(2):
            ru = slice(128 * u, 128 * u + 128)
            q = qkv[0, ru, hc]
            s_l = nt(q, qkv[1, ru, hc]) * (SCALE * LOG2E) + bias_l[ru]
            s_b = nt(q, kb) * (SCALE * LOG2E)
            s_m = s_b[:, :128] + bias_m[e, ru]
            s_f = s_b[:, 128:] + bias_f[hh, ru]
            top = jnp.max(jnp.maximum(jnp.maximum(s_l, s_m), s_f), axis=1, keepdims=True)
            e_l, e_m, e_f = jnp.exp2(s_l - top), jnp.exp2(s_m - top), jnp.exp2(s_f - top)
            inv = 1.0 / jnp.sum(e_l + e_m + e_f, axis=1, keepdims=True)
            p_l = (e_l * inv).astype(BF)
            p_b = jnp.concatenate([(e_m * inv).astype(BF), (e_f * inv).astype(BF)], axis=1)
            probs[hh, ru, :128] = p_l
            probs[hh, ru, 128:] = p_b
            mixc[ru, hc] = (nn(p_l, qkv[2, ru, hc]) + nn(p_b, vb)).astype(BF)
        return carry

    lax.fori_loop(0, 8, forward, 0, unroll=4)

    mix_sent = []
    for g, (a, peer, first) in enumerate(((x, x_peer, 0), (y, y_peer, x))):
        mx_g[g][a] = mixc[:, times(256 * lax.rem(first + a, 4), 256)]
        mix_sent.append(
            [
                Sent(mixc.at[:, times(256 * lax.rem(first + a + k, 4), 256)], mx_g[g].at[a], peer(k))
                for k in (1, 2, 3)
            ]
        )
    swap_mx = [
        Sent(mixc.at[theirs, block(b)], mx.at[:, mine(b)], partner) for b in range(4)
    ]
    for b in range(4):
        mx[:, mine(b)] = mixc[own, 256 * b : 256 * b + 256]

    relay_x = relay(0, gather_x)
    forwarded += [to_partner(0, k) for k in (1, 3)]

    def backward(hh, carry):
        hc = times(hh * HD, HD)
        kb, vb = kvb[0, :, hc], kvb[1, :, hc]
        ds_rows = []
        for u in range(2):
            ru = slice(128 * u, 128 * u + 128)
            q, k, v = qkv[0, ru, hc], qkv[1, ru, hc], qkv[2, ru, hc]
            gr = mg[ru, hc]
            delta = jnp.sum(gr.astype(F32) * mixc[ru, hc].astype(F32), axis=1, keepdims=True)
            p_l, p_b = probs[hh, ru, :128], probs[hh, ru, 128:]
            ds_l = (p_l.astype(F32) * (nt(gr, v) - delta)).astype(BF)
            ds_b = (p_b.astype(F32) * (nt(gr, vb) - delta)).astype(BF)
            dqb[ru, hc] = ((nn(ds_l, k) + nn(ds_b, kb)) * SCALE).astype(BF)
            dkv[0, ru, hc] = tn(ds_l, q)
            dkv[1, ru, hc] = tn(p_l, gr)
            ds_rows.append(ds_b)
        sb[0, :, hc] = tn(jnp.concatenate(ds_rows, axis=0), qkv[0, :, hc]).astype(BF)
        sb[1, :, hc] = tn(probs[hh, :, 128:], mg[:, hc]).astype(BF)
        return carry

    lax.fori_loop(0, 8, backward, 0, unroll=4)

    mid_back = Sent(sb.at[:, times(64 * (1 - zl), 64)], rm, neighbour)
    far_back = [
        Sent(sb.at[:, pl.ds(pl.multiple_of(128 + 32 * lax.rem(x + k, 4), 32), 32)], rfx.at[k - 1], x_peer(k))
        for k in (1, 2, 3)
    ]

    def give(buf, out):
        for b in range(4):
            Local(buf.at[own, block(b)], out.at[:, mine(b)])
            Sent(buf.at[theirs, block(b)], out.at[:, mine(b)], partner)

    for g, passed in ((1, relay_y), (0, relay_x)):
        for copy in passed:
            copy.wait_recv()
        forwarded.append(to_partner(g, 2))
    give(dqb, dq_out)

    for copy in forwarded:
        copy.wait_recv()
    around = (z, z_peer), (x, diagonal_peer)
    turned = []
    for g in range(2):
        for copy in mix_sent[g]:
            copy.wait_recv()
        turned.append(mx_g[g][...].reshape(HALF, 256).T)
    sent_1 = []
    for g, n in UNITS:
        for c0 in range(PART * n, PART * n + PART, 256):
            cols = slice(c0, c0 + 256)
            t_g[g][:, cols] = nn(turned[g], og_g[g][:, :, cols].reshape(HALF, 256)).astype(BF)
        cols = pl.ds(PART * n, PART)
        a, peer = around[g]
        sent_1.append(
            [
                Sent(t_g[g].at[times(64 * lax.rem(a + k, 4), 64), cols], r1_g[g].at[k - 1, :, cols], peer(k))
                for k in (1, 2, 3)
            ]
        )

    for copy in in_w2:
        copy.wait()
    for copy in swap_mx:
        copy.wait_recv()

    def out_block(n, carry):
        cols = times(n * 512, 512)
        lob[:, cols] = nn(mx[...], wo[:, cols]).astype(BF)
        return carry

    lax.fori_loop(0, 4, out_block, 0)
    Local(lob, lo_out)

    for copy in far_back:
        copy.wait_recv()
    far_sum[...] = sb[:, pl.ds(pl.multiple_of(128 + 32 * x, 32), 32)].astype(F32)
    for k in range(3):
        far_sum[...] += rfx[k].astype(F32)
    fs[...] = far_sum[:, times(16 * (1 - zl), 16)].astype(BF)
    far_last = Sent(fs, rfz, neighbour)

    around_2 = (y, y_peer), (z, z_peer)
    sent_2 = []
    for (g, n), copies in zip(UNITS, sent_1):
        for copy in copies:
            copy.wait_recv()
        cols = slice(PART * n, PART * n + PART)
        total = t_g[g][times(64 * around[g][0], 64), cols].astype(F32)
        for k in range(3):
            total = total + r1_g[g][k, :, cols].astype(F32)
        s2_g[g][:, cols] = total.astype(BF)
        cols = pl.ds(PART * n, PART)
        a, peer = around_2[g]
        sent_2.append(
            [
                Sent(s2_g[g].at[times(16 * lax.rem(a + k, 4), 16), cols], r2_g[g].at[k - 1, :, cols], peer(k))
                for k in (1, 2, 3)
            ]
        )

    mid_back.wait_recv()
    far_last.wait_recv()
    far_mine = times(16 * zl, 16)
    for i, out in ((0, dk_out), (1, dv_out)):
        spread[...] = jnp.zeros_like(spread)
        for hh in range(8):
            hc = slice(HD * hh, HD * hh + HD)
            e = hh % 2
            spread[64 * e : 64 * e + 64, hc] = (
                sb[i, mid_own, hc].astype(F32) + rm[i, :, hc].astype(F32)
            ).astype(BF)
            spread[128 + 16 * hh : 144 + 16 * hh, hc] = (
                far_sum[i, far_mine, hc] + rfz[i, :, hc].astype(F32)
            ).astype(BF)
        total = dkv[i] + tn(sel[...], spread[...])
        outs[i] = (total * SCALE if i == 0 else total).astype(BF)
        give(outs.at[i], out)

    piece = lax.rem(4 * zl + y, 8), lax.rem(4 * lax.rem(x, 2) + z, 8)
    owners = owner_x, owner_y
    for m, ((g, n), copies) in enumerate(zip(UNITS, sent_2)):
        for copy in copies:
            copy.wait_recv()
        cols = slice(PART * n, PART * n + PART)
        total = s2_g[g][times(16 * around_2[g][0], 16), cols].astype(F32)
        for k in range(3):
            total = total + r2_g[g][k, :, cols].astype(F32)
        s3_g[g][:, cols] = total.astype(BF)
        src = s3_g[g].at[:, pl.ds(PART * n, PART)]
        dst = wgr.at[times(16 * piece[g], 16), pl.ds(GATHERS[g][1] + PART * n, PART)]
        for dp in range(8):
            stays = jnp.logical_and(owners[g] == c, d == dp)

            @pl.when(stays)
            def _(m=m, g=g, src=src, dst=dst):
                pltpu.make_async_copy(src, dst, last_recv.at[8 * m + piece[g]]).start()

            @pl.when(jnp.logical_not(stays))
            def _(m=m, g=g, dp=dp, src=src, dst=dst):
                pltpu.make_async_remote_copy(
                    src_ref=src,
                    dst_ref=dst,
                    send_sem=last_send.at[8 * m + dp],
                    recv_sem=last_recv.at[8 * m + piece[g]],
                    device_id=(owners[g], jnp.int32(dp)),
                    device_id_type=MESH,
                ).start()

    for m, (g, n) in enumerate(UNITS):
        src = s3_g[g].at[:, pl.ds(PART * n, PART)]
        for k in range(8):
            ref = wgr.at[pl.ds(16 * k, 16), pl.ds(GATHERS[g][1] + PART * n, PART)]
            pltpu.make_async_copy(src, ref, last_recv.at[8 * m + k]).wait()
    Local(wgr, wg_out)

    for m, (g, n) in enumerate(UNITS):
        src = s3_g[g].at[:, pl.ds(PART * n, PART)]
        for dp in range(8):

            @pl.when(jnp.logical_not(jnp.logical_and(owners[g] == c, d == dp)))
            def _(m=m, dp=dp, src=src):
                pltpu.make_async_copy(src, src, last_send.at[8 * m + dp]).wait()

    drain()


def place(lo, dq, dk, dv, wg, lo_out, dq_out, dk_out, dv_out, wg_out, held, wg32, sems):
    pairs = ((wg, None), (lo, lo_out), (dq, dq_out), (dk, dk_out), (dv, dv_out))
    taken = [pltpu.make_async_copy(src, held.at[n], sems.at[n]) for n, (src, _) in enumerate(pairs)]
    for copy in taken:
        copy.start()
    given = []
    for n, (_, dst) in enumerate(pairs):
        taken[n].wait()
        if dst is None:
            wg32[...] = held[n].astype(F32)
        given.append(
            pltpu.make_async_copy(wg32 if dst is None else held.at[n], wg_out if dst is None else dst, sems.at[5 + n])
        )
        given[n].start()
    for copy in given:
        copy.wait()


def shards(queries, key_states, value_states, out_grad, w_out, doc_lengths):
    rows = queries.shape[1]
    hbm = pl.BlockSpec(memory_space=pl.ANY)
    out16 = jax.ShapeDtypeStruct((rows, WIDTH), BF)
    vm = pltpu.VMEM
    outs = pl.pallas_call(
        kernel,
        out_shape=[out16] * 5,
        in_specs=[pl.BlockSpec(memory_space=pltpu.SMEM)] + [hbm] * 5,
        out_specs=[hbm] * 5,
        scratch_shapes=[
            vm((3, 256, HALF), BF),
            vm((2, 256, HALF), BF),
            vm((4, 256, HALF), BF),
            vm((4, 256, HALF), BF),
            vm((WIDTH, WIDTH), BF),
            vm((256, HALF), BF),
            vm((256, HALF), BF),
            vm((4, 256, 256), BF),
            vm((4, 256, 256), BF),
            vm((128, WIDTH), BF),
            vm((8, 256, 384), BF),
            vm((256, 128), F32),
            vm((2, 256, 128), F32),
            vm((8, 256, 128), F32),
            vm((256, 256), BF),
            vm((2, 256, HALF), F32),
            vm((256, HALF), BF),
            vm((2, 256, HALF), BF),
            vm((2, 64, HALF), BF),
            vm((3, 2, 32, HALF), BF),
            vm((2, 16, HALF), BF),
            vm((2, 16, HALF), BF),
            vm((2, 32, HALF), F32),
            vm((256, HALF), BF),
            vm((2, 256, HALF), BF),
            vm((128, WIDTH), BF),
            vm((256, HALF), BF),
            vm((256, HALF), BF),
            vm((3, 64, HALF), BF),
            vm((3, 64, HALF), BF),
            vm((64, HALF), BF),
            vm((64, HALF), BF),
            vm((3, 16, HALF), BF),
            vm((3, 16, HALF), BF),
            vm((16, HALF), BF),
            vm((16, HALF), BF),
            vm((128, WIDTH), BF),
            pltpu.SemaphoreType.DMA((96,)),
            pltpu.SemaphoreType.DMA((96,)),
            pltpu.SemaphoreType.DMA((40,)),
            pltpu.SemaphoreType.DMA((32,)),
            pltpu.SemaphoreType.DMA((32,)),
        ],
        compiler_params=pltpu.CompilerParams(
            collective_id=0, has_side_effects=True, vmem_limit_bytes=56 << 20
        ),
        name="dilated_attention",
    )(doc_lengths, queries[0], key_states[0], value_states[0], out_grad[0], w_out)
    outs = pl.pallas_call(
        place,
        out_shape=[out16] * 4 + [jax.ShapeDtypeStruct((rows, WIDTH), F32)],
        in_specs=[hbm] * 5,
        out_specs=[hbm] * 5,
        scratch_shapes=[vm((5, rows, WIDTH), BF), vm((rows, WIDTH), F32), pltpu.SemaphoreType.DMA((10,))],
        name="place_results",
    )(*outs)
    return tuple(o[None] for o in outs[:4]) + (outs[4],)


def solution(mesh):
    rows = P("dp", "ctx", None)
    return jax.shard_map(
        shards,
        mesh=mesh,
        in_specs=(rows, rows, rows, rows, P(), P("dp", None)),
        out_specs=(rows, rows, rows, rows, P("ctx", None)),
        check_vma=False,
    )
```

```python
import functools

import jax
import jax.numpy as jnp
from jax import lax
from jax.experimental import pallas as pl
from jax.experimental.pallas import tpu as pltpu
from jax.sharding import PartitionSpec as P

MESH = pl.DeviceIdType.MESH
BF, F32 = jnp.bfloat16, jnp.float32
HD = 128
SCALE = HD**-0.5
LOG2E = 1.4426950408889634
HIDE = -1e30
WIDTH = 2048
HALF = 1024
GATHERS = (("x", 0, HALF), ("y", HALF, HALF))
PART = 512
UNITS = [(g, n) for n in range(HALF // PART) for g in range(2)]


def nn(a, b):
    return lax.dot_general(a, b, (((1,), (0,)), ((), ())), preferred_element_type=F32)


def nt(a, b):
    return lax.dot_general(a, b, (((1,), (1,)), ((), ())), preferred_element_type=F32)


def tn(a, b):
    return lax.dot_general(a, b, (((0,), (0,)), ((), ())), preferred_element_type=F32)


def times(n, step):
    return pl.ds(pl.multiple_of(n, step), step)


def kernel(
    docs,
    q_hbm,
    k_hbm,
    v_hbm,
    og_hbm,
    w_hbm,
    lo_out,
    dq_out,
    dk_out,
    dv_out,
    wg_out,
    qkv,
    kvb,
    og_x,
    og_y,
    wo,
    mg,
    mixc,
    mx_x,
    mx_y,
    mx,
    probs,
    bias_l,
    bias_m,
    bias_f,
    sel,
    dkv,
    dqb,
    sb,
    rm,
    rfx,
    fs,
    rfz,
    far_sum,
    spread,
    outs,
    lob,
    t_x,
    t_y,
    r1_x,
    r1_y,
    s2_x,
    s2_y,
    r2_x,
    r2_y,
    s3_x,
    s3_y,
    wgr,
    send_sem,
    recv_sem,
    local_sem,
    last_send,
    last_recv,
):
    c, d = lax.axis_index("ctx"), lax.axis_index("dp")
    x, zl, j = lax.div(c, 4), lax.rem(lax.div(c, 2), 2), lax.rem(c, 2)
    zh, y = lax.div(d, 4), lax.rem(d, 4)
    z = zh * 2 + zl
    og_g, mx_g, t_g = (og_x, og_y), (mx_x, mx_y), (t_x, t_y)
    r1_g, s2_g, r2_g, s3_g = (r1_x, r1_y), (s2_x, s2_y), (r2_x, r2_y), (s3_x, s3_y)

    def at(x_=None, zl_=None, j_=None, zh_=None, y_=None):
        cx = (x if x_ is None else x_) * 4 + (zl if zl_ is None else zl_) * 2 + (j if j_ is None else j_)
        return (cx, (zh if zh_ is None else zh_) * 4 + (y if y_ is None else y_))

    def diagonal_peer(k):
        return at(x_=lax.rem(x + k, 4), y_=lax.rem(y + 4 - k, 4))

    def x_peer(k):
        return at(x_=lax.rem(x + k, 4))

    def y_peer(k):
        return at(y_=lax.rem(y + k, 4))

    def z_peer(k):
        other = lax.rem(z + k, 4)
        return at(zl_=lax.rem(other, 2), zh_=lax.div(other, 2))

    partner, neighbour = at(j_=1 - j), at(zl_=1 - zl)
    in_flight = []

    class Sent:
        def __init__(self, src, dst, device):
            n = sum(isinstance(copy, Sent) for copy in in_flight)
            in_flight.append(self)
            self.landed = False
            self.copy = pltpu.make_async_remote_copy(
                src_ref=src,
                dst_ref=dst,
                send_sem=send_sem.at[n],
                recv_sem=recv_sem.at[n],
                device_id=device,
                device_id_type=MESH,
            )
            self.copy.start()

        def wait_recv(self):
            if not self.landed:
                self.landed = True
                self.copy.wait_recv()

        def finish(self):
            self.wait_recv()
            self.copy.wait_send()

    class Local:
        def __init__(self, src, dst):
            n = sum(isinstance(copy, Local) for copy in in_flight)
            in_flight.append(self)
            self.done = False
            self.copy = pltpu.make_async_copy(src, dst, local_sem.at[n])
            self.copy.start()

        def wait(self):
            if not self.done:
                self.done = True
                self.copy.wait()

        finish = wait

    def drain():
        for copy in in_flight:
            copy.finish()

    own = times(j * 128, 128)
    theirs = times((1 - j) * 128, 128)

    def mine(b):
        return times(256 * (2 * b + j), 256)

    def not_mine(b):
        return times(256 * (2 * b + 1 - j), 256)

    def block(b):
        return pl.ds(256 * b, 256)

    in_kv = [
        Local(hbm.at[:, mine(b)], qkv.at[i, own, block(b)])
        for i, hbm in ((1, k_hbm), (2, v_hbm))
        for b in range(4)
    ]
    in_og = [
        Local(og_hbm.at[:, pl.ds(c0, nc)], og_g[g].at[a, own])
        for g, (a, (_, c0, nc)) in enumerate(zip((x, y), GATHERS))
    ]
    in_w = [Local(w_hbm.at[mine(b)], wo.at[mine(b)]) for b in range(4)]
    in_q = [Local(q_hbm.at[:, mine(b)], qkv.at[0, own, block(b)]) for b in range(4)]
    in_w2 = [Local(w_hbm.at[not_mine(b)], wo.at[not_mine(b)]) for b in range(4)]

    barrier = pltpu.get_barrier_semaphore()
    near = [partner] + [
        peer(k) for peer in (x_peer, y_peer, z_peer, diagonal_peer) for k in (1, 2, 3)
    ]
    for device in near:
        pl.semaphore_signal(barrier, inc=1, device_id=device, device_id_type=MESH)
    for n in range(8):
        a, b = 2 * j + n // 4, n % 4
        from_x = at(zl_=n // 4, j_=zl, zh_=j, y_=b)
        from_y = at(x_=a, zl_=b % 2, j_=zl, zh_=b // 2, y_=lax.rem(x + 4 - a, 4))
        for cc, dd in (from_x, from_y):

            @pl.when(jnp.logical_or(cc != c, dd != d))
            def _(cc=cc, dd=dd):
                pl.semaphore_signal(barrier, inc=1, device_id=(cc, dd), device_id_type=MESH)

    owner_x = x * 4 + j * 2 + zh
    owner_y = lax.rem(x + y, 4) * 4 + j * 2 + lax.div(x, 2)
    away = 16 - (owner_x == c).astype(jnp.int32) - (owner_y == c).astype(jnp.int32)
    pl.semaphore_wait(barrier, len(near) + away)

    swap_kv = [
        Sent(hbm.at[:, not_mine(b)], qkv.at[i, own, block(b)], partner)
        for i, hbm in ((1, k_hbm), (2, v_hbm))
        for b in range(4)
    ]
    swap_og = [
        Sent(og_hbm.at[:, pl.ds(c0, nc)], og_g[g].at[a, own], partner)
        for g, (a, (_, c0, nc)) in enumerate(zip((x, y), GATHERS))
    ]
    swap_q = [Sent(q_hbm.at[:, not_mine(b)], qkv.at[0, own, block(b)], partner) for b in range(4)]

    def gather(g):
        a, peer = ((x, x_peer), (y, y_peer))[g]
        _, c0, nc = GATHERS[g]
        return [Sent(og_hbm.at[:, pl.ds(c0, nc)], og_g[g].at[a, own], peer(k)) for k in (1, 3)]

    def relay(g, copies):
        a, peer = ((x, x_peer), (y, y_peer))[g]
        passed = []
        for n, (k, copy) in enumerate(zip((1, 3), copies)):
            copy.wait_recv()
            ref = og_g[g].at[lax.rem(a + 4 - k, 4), pl.ds(pl.multiple_of(128 * j + 64 * n, 64), 64)]
            passed.append(Sent(ref, ref, peer(k)))
        return passed

    def to_partner(g, k):
        a = (x, y)[g]
        ref = og_g[g].at[lax.rem(a + k, 4), own]
        return Sent(ref, ref, partner)

    gather_y = gather(1)

    row = lax.broadcasted_iota(jnp.int32, (256, 256), 0)
    col = lax.broadcasted_iota(jnp.int32, (256, 256), 1)
    far_head = lax.shift_right_logical(row - 128, 4)
    mid_row = 4 * (row & 63) + 2 * j + (lax.shift_right_logical(row, 6) & 1)
    far_row = 16 * (row & 15) + 4 * lax.shift_right_logical(far_head, 1) + 2 * j + (far_head & 1)
    sel[...] = (col == jnp.where(row < 128, mid_row, far_row)).astype(F32).astype(BF)

    far_own = pl.ds(pl.multiple_of(128 + 16 * (2 * x + zl), 16), 16)
    far_near = pl.ds(pl.multiple_of(128 + 16 * (2 * x + 1 - zl), 16), 16)
    mid_own = times(64 * zl, 64)
    for i in (0, 1):
        for copy in in_kv[4 * i : 4 * i + 4]:
            copy.wait()
        for copy in swap_kv[4 * i : 4 * i + 4]:
            copy.wait_recv()
        picked = nn(sel[...], qkv[1 + i]).astype(BF)
        for hh in range(8):
            hc = slice(HD * hh, HD * hh + HD)
            e = hh % 2
            kvb[i, mid_own, hc] = picked[64 * e : 64 * e + 64, hc]
            kvb[i, far_own, hc] = picked[128 + 16 * hh : 144 + 16 * hh, hc]
    far_z = Sent(kvb.at[:, far_own], kvb.at[:, far_own], neighbour)
    far_x = [Sent(kvb.at[:, far_own], kvb.at[:, far_own], x_peer(k)) for k in (1, 2, 3)]

    mid_sent = [Sent(kvb.at[:, mid_own], kvb.at[:, mid_own], neighbour)]
    base = x * 512 + zl * 256
    here = lax.broadcasted_iota(jnp.int32, (256, 128), 0)
    key = lax.broadcasted_iota(jnp.int32, (256, 128), 1)
    pos = base + here
    start = jnp.zeros((256, 128), jnp.int32)
    end = jnp.int32(0)
    for n in range(8):
        end = end + docs[0, n]
        start = jnp.where(pos >= end, end, start)

    def shown(key_pos, extra):
        seen = jnp.logical_and(key_pos <= pos, key_pos >= start)
        if extra is not None:
            seen = jnp.logical_and(seen, extra)
        return jnp.where(seen, 0.0, HIDE).astype(F32)

    bias_l[...] = shown(base + (here & 128) + key, None)
    for e in range(2):
        r = 2 * j + e
        bias_m[e] = shown(x * 512 + 4 * key + r, (here & 3) == r)
    for hh in range(8):
        h = 4 * (hh // 2) + 2 * j + hh % 2
        bias_f[hh] = shown(16 * key + h, (here & 15) == h)

    for copy in in_og:
        copy.wait()
    for copy in swap_og:
        copy.wait_recv()

    def mixed_grad_block(b):
        in_w[b].wait()
        part = nt(og_x[x], wo[mine(b), :HALF]) + nt(og_y[y], wo[mine(b), HALF:])
        mg[:, 256 * b : 256 * b + 256] = part.astype(BF)

    mixed_grad_block(0)
    far_z.wait_recv()
    far_fwd = [Sent(kvb.at[:, far_near], kvb.at[:, far_near], x_peer(k)) for k in (1, 2, 3)]
    gather_x = gather(0)
    for b in (1, 2, 3):
        mixed_grad_block(b)
    relay_y = relay(1, gather_y)
    forwarded = [to_partner(1, k) for k in (1, 3)]
    for copy in in_q:
        copy.wait()
    for copy in swap_q + mid_sent + far_x + far_fwd:
        copy.wait_recv()

    def halves(f, *operands):
        return jnp.concatenate([f(*(o[:128] for o in operands)), f(*(o[128:] for o in operands))], axis=0)

    def forward(hh, carry):
        hc = times(hh * HD, HD)
        q = qkv[0, :, hc]
        s_l = halves(nt, q, qkv[1, :, hc]) * (SCALE * LOG2E) + bias_l[...]
        s_b = nt(q, kvb[0, :, hc]) * (SCALE * LOG2E)
        s_m = s_b[:, :128] + bias_m[lax.rem(hh, 2)]
        s_f = s_b[:, 128:] + bias_f[hh]
        top = jnp.max(jnp.maximum(jnp.maximum(s_l, s_m), s_f), axis=1, keepdims=True)
        e_l, e_m, e_f = jnp.exp2(s_l - top), jnp.exp2(s_m - top), jnp.exp2(s_f - top)
        inv = 1.0 / jnp.sum(e_l + e_m + e_f, axis=1, keepdims=True)
        p_l = (e_l * inv).astype(BF)
        p_b = jnp.concatenate([(e_m * inv).astype(BF), (e_f * inv).astype(BF)], axis=1)
        probs[hh, :, :128] = p_l
        probs[hh, :, 128:] = p_b
        mixc[:, hc] = (halves(nn, p_l, qkv[2, :, hc]) + nn(p_b, kvb[1, :, hc])).astype(BF)
        return carry

    lax.fori_loop(0, 8, forward, 0, unroll=4)

    mix_sent = []
    for g, (a, peer, first) in enumerate(((x, x_peer, 0), (y, y_peer, x))):
        mx_g[g][a] = mixc[:, times(256 * lax.rem(first + a, 4), 256)]
        mix_sent.append(
            [
                Sent(mixc.at[:, times(256 * lax.rem(first + a + k, 4), 256)], mx_g[g].at[a], peer(k))
                for k in (1, 2, 3)
            ]
        )
    swap_mx = [
        Sent(mixc.at[theirs, block(b)], mx.at[:, mine(b)], partner) for b in range(4)
    ]
    for b in range(4):
        mx[:, mine(b)] = mixc[own, 256 * b : 256 * b + 256]

    relay_x = relay(0, gather_x)
    forwarded += [to_partner(0, k) for k in (1, 3)]

    def backward(hh, carry):
        hc = times(hh * HD, HD)
        q, gr = qkv[0, :, hc], mg[:, hc]
        delta = jnp.sum(gr.astype(F32) * mixc[:, hc].astype(F32), axis=1, keepdims=True)
        p_l, p_b = probs[hh, :, :128], probs[hh, :, 128:]
        ds_l = (p_l.astype(F32) * (halves(nt, gr, qkv[2, :, hc]) - delta)).astype(BF)
        ds_b = (p_b.astype(F32) * (nt(gr, kvb[1, :, hc]) - delta)).astype(BF)
        dq = halves(nn, ds_l, qkv[1, :, hc]) + nn(ds_b, kvb[0, :, hc])
        dqb[:, hc] = (dq * SCALE).astype(BF)
        dkv[0, :, hc] = halves(tn, ds_l, q)
        dkv[1, :, hc] = halves(tn, p_l, gr)
        sb[0, :, hc] = tn(ds_b, q).astype(BF)
        sb[1, :, hc] = tn(p_b, gr).astype(BF)
        return carry

    lax.fori_loop(0, 8, backward, 0, unroll=4)

    mid_back = Sent(sb.at[:, times(64 * (1 - zl), 64)], rm, neighbour)
    far_back = [
        Sent(sb.at[:, pl.ds(pl.multiple_of(128 + 32 * lax.rem(x + k, 4), 32), 32)], rfx.at[k - 1], x_peer(k))
        for k in (1, 2, 3)
    ]

    def give(buf, out):
        for b in range(4):
            Local(buf.at[own, block(b)], out.at[:, mine(b)])
            Sent(buf.at[theirs, block(b)], out.at[:, mine(b)], partner)

    for g, passed in ((1, relay_y), (0, relay_x)):
        for copy in passed:
            copy.wait_recv()
        forwarded.append(to_partner(g, 2))
    give(dqb, dq_out)

    for copy in forwarded:
        copy.wait_recv()
    around = (z, z_peer), (x, diagonal_peer)
    turned = []
    for g in range(2):
        for copy in mix_sent[g]:
            copy.wait_recv()
        turned.append(mx_g[g][...].reshape(HALF, 256).T)
    sent_1 = []
    for g, n in UNITS:
        for c0 in range(PART * n, PART * n + PART, 256):
            cols = slice(c0, c0 + 256)
            t_g[g][:, cols] = nn(turned[g], og_g[g][:, :, cols].reshape(HALF, 256)).astype(BF)
        cols = pl.ds(PART * n, PART)
        a, peer = around[g]
        sent_1.append(
            [
                Sent(t_g[g].at[times(64 * lax.rem(a + k, 4), 64), cols], r1_g[g].at[k - 1, :, cols], peer(k))
                for k in (1, 2, 3)
            ]
        )

    for copy in in_w2:
        copy.wait()
    for copy in swap_mx:
        copy.wait_recv()

    def out_block(n, carry):
        cols = times(n * 512, 512)
        lob[:, cols] = nn(mx[...], wo[:, cols]).astype(BF)
        return carry

    lax.fori_loop(0, 4, out_block, 0)
    Local(lob, lo_out)

    for copy in far_back:
        copy.wait_recv()
    far_sum[...] = sb[:, pl.ds(pl.multiple_of(128 + 32 * x, 32), 32)].astype(F32)
    for k in range(3):
        far_sum[...] += rfx[k].astype(F32)
    fs[...] = far_sum[:, times(16 * (1 - zl), 16)].astype(BF)
    far_last = Sent(fs, rfz, neighbour)

    around_2 = (y, y_peer), (z, z_peer)
    sent_2 = []
    for (g, n), copies in zip(UNITS, sent_1):
        for copy in copies:
            copy.wait_recv()
        cols = slice(PART * n, PART * n + PART)
        total = t_g[g][times(64 * around[g][0], 64), cols].astype(F32)
        for k in range(3):
            total = total + r1_g[g][k, :, cols].astype(F32)
        s2_g[g][:, cols] = total.astype(BF)
        cols = pl.ds(PART * n, PART)
        a, peer = around_2[g]
        sent_2.append(
            [
                Sent(s2_g[g].at[times(16 * lax.rem(a + k, 4), 16), cols], r2_g[g].at[k - 1, :, cols], peer(k))
                for k in (1, 2, 3)
            ]
        )

    piece = lax.rem(4 * zl + y, 8), lax.rem(4 * lax.rem(x, 2) + z, 8)
    owners = owner_x, owner_y
    for m, ((g, n), copies) in enumerate(zip(UNITS, sent_2)):
        for copy in copies:
            copy.wait_recv()
        cols = slice(PART * n, PART * n + PART)
        total = s2_g[g][times(16 * around_2[g][0], 16), cols].astype(F32)
        for k in range(3):
            total = total + r2_g[g][k, :, cols].astype(F32)
        s3_g[g][:, cols] = total.astype(BF)
        src = s3_g[g].at[:, pl.ds(PART * n, PART)]
        dst = wgr.at[times(16 * piece[g], 16), pl.ds(GATHERS[g][1] + PART * n, PART)]
        for dp in range(8):
            stays = jnp.logical_and(owners[g] == c, d == dp)

            @pl.when(stays)
            def _(m=m, g=g, src=src, dst=dst):
                pltpu.make_async_copy(src, dst, last_recv.at[8 * m + piece[g]]).start()

            @pl.when(jnp.logical_not(stays))
            def _(m=m, g=g, dp=dp, src=src, dst=dst):
                pltpu.make_async_remote_copy(
                    src_ref=src,
                    dst_ref=dst,
                    send_sem=last_send.at[8 * m + dp],
                    recv_sem=last_recv.at[8 * m + piece[g]],
                    device_id=(owners[g], jnp.int32(dp)),
                    device_id_type=MESH,
                ).start()

    mid_back.wait_recv()
    far_last.wait_recv()
    far_mine = times(16 * zl, 16)
    for i, out in ((0, dk_out), (1, dv_out)):
        spread[...] = jnp.zeros_like(spread)
        for hh in range(8):
            hc = slice(HD * hh, HD * hh + HD)
            e = hh % 2
            spread[64 * e : 64 * e + 64, hc] = (
                sb[i, mid_own, hc].astype(F32) + rm[i, :, hc].astype(F32)
            ).astype(BF)
            spread[128 + 16 * hh : 144 + 16 * hh, hc] = (
                far_sum[i, far_mine, hc] + rfz[i, :, hc].astype(F32)
            ).astype(BF)
        total = dkv[i] + tn(sel[...], spread[...])
        outs[i] = (total * SCALE if i == 0 else total).astype(BF)
        give(outs.at[i], out)

    for m, (g, n) in enumerate(UNITS):
        src = s3_g[g].at[:, pl.ds(PART * n, PART)]
        for k in range(8):
            ref = wgr.at[pl.ds(16 * k, 16), pl.ds(GATHERS[g][1] + PART * n, PART)]
            pltpu.make_async_copy(src, ref, last_recv.at[8 * m + k]).wait()
    Local(wgr, wg_out)

    for m, (g, n) in enumerate(UNITS):
        src = s3_g[g].at[:, pl.ds(PART * n, PART)]
        for dp in range(8):

            @pl.when(jnp.logical_not(jnp.logical_and(owners[g] == c, d == dp)))
            def _(m=m, dp=dp, src=src):
                pltpu.make_async_copy(src, src, last_send.at[8 * m + dp]).wait()

    drain()


def place(lo, dq, dk, dv, wg, lo_out, dq_out, dk_out, dv_out, wg_out, held, wg32, sems):
    pairs = ((wg, None), (lo, lo_out), (dq, dq_out), (dk, dk_out), (dv, dv_out))
    taken = [pltpu.make_async_copy(src, held.at[n], sems.at[n]) for n, (src, _) in enumerate(pairs)]
    for copy in taken:
        copy.start()
    given = []
    for n, (_, dst) in enumerate(pairs):
        taken[n].wait()
        if dst is None:
            wg32[...] = held[n].astype(F32)
        given.append(
            pltpu.make_async_copy(wg32 if dst is None else held.at[n], wg_out if dst is None else dst, sems.at[5 + n])
        )
        given[n].start()
    for copy in given:
        copy.wait()


def shards(queries, key_states, value_states, out_grad, w_out, doc_lengths):
    rows = queries.shape[1]
    hbm = pl.BlockSpec(memory_space=pl.ANY)
    out16 = jax.ShapeDtypeStruct((rows, WIDTH), BF)
    vm = pltpu.VMEM
    outs = pl.pallas_call(
        kernel,
        out_shape=[out16] * 5,
        in_specs=[pl.BlockSpec(memory_space=pltpu.SMEM)] + [hbm] * 5,
        out_specs=[hbm] * 5,
        scratch_shapes=[
            vm((3, 256, HALF), BF),
            vm((2, 256, HALF), BF),
            vm((4, 256, HALF), BF),
            vm((4, 256, HALF), BF),
            vm((WIDTH, WIDTH), BF),
            vm((256, HALF), BF),
            vm((256, HALF), BF),
            vm((4, 256, 256), BF),
            vm((4, 256, 256), BF),
            vm((128, WIDTH), BF),
            vm((8, 256, 384), BF),
            vm((256, 128), F32),
            vm((2, 256, 128), F32),
            vm((8, 256, 128), F32),
            vm((256, 256), BF),
            vm((2, 256, HALF), F32),
            vm((256, HALF), BF),
            vm((2, 256, HALF), BF),
            vm((2, 64, HALF), BF),
            vm((3, 2, 32, HALF), BF),
            vm((2, 16, HALF), BF),
            vm((2, 16, HALF), BF),
            vm((2, 32, HALF), F32),
            vm((256, HALF), BF),
            vm((2, 256, HALF), BF),
            vm((128, WIDTH), BF),
            vm((256, HALF), BF),
            vm((256, HALF), BF),
            vm((3, 64, HALF), BF),
            vm((3, 64, HALF), BF),
            vm((64, HALF), BF),
            vm((64, HALF), BF),
            vm((3, 16, HALF), BF),
            vm((3, 16, HALF), BF),
            vm((16, HALF), BF),
            vm((16, HALF), BF),
            vm((128, WIDTH), BF),
            pltpu.SemaphoreType.DMA((96,)),
            pltpu.SemaphoreType.DMA((96,)),
            pltpu.SemaphoreType.DMA((40,)),
            pltpu.SemaphoreType.DMA((32,)),
            pltpu.SemaphoreType.DMA((32,)),
        ],
        compiler_params=pltpu.CompilerParams(
            collective_id=0, has_side_effects=True, vmem_limit_bytes=56 << 20
        ),
        name="dilated_attention",
    )(doc_lengths, queries[0], key_states[0], value_states[0], out_grad[0], w_out)
    outs = pl.pallas_call(
        place,
        out_shape=[out16] * 4 + [jax.ShapeDtypeStruct((rows, WIDTH), F32)],
        in_specs=[hbm] * 5,
        out_specs=[hbm] * 5,
        scratch_shapes=[vm((5, rows, WIDTH), BF), vm((rows, WIDTH), F32), pltpu.SemaphoreType.DMA((10,))],
        name="place_results",
    )(*outs)
    return tuple(o[None] for o in outs[:4]) + (outs[4],)


def solution(mesh):
    rows = P("dp", "ctx", None)
    return jax.shard_map(
        shards,
        mesh=mesh,
        in_specs=(rows, rows, rows, rows, P(), P("dp", None)),
        out_specs=(rows, rows, rows, rows, P("ctx", None)),
        check_vma=False,
    )
```

```python
import functools

import jax
import jax.numpy as jnp
from jax import lax
from jax.experimental import pallas as pl
from jax.experimental.pallas import tpu as pltpu
from jax.sharding import PartitionSpec as P

MESH = pl.DeviceIdType.MESH
BF, F32 = jnp.bfloat16, jnp.float32
HD = 128
SCALE = HD**-0.5
LOG2E = 1.4426950408889634
HIDE = -1e30
WIDTH = 2048
HALF = 1024
GATHERS = (("x", 0, HALF), ("y", HALF, HALF))
PART = 512
UNITS = [(g, n) for n in range(HALF // PART) for g in range(2)]


def nn(a, b):
    return lax.dot_general(a, b, (((1,), (0,)), ((), ())), preferred_element_type=F32)


def nt(a, b):
    return lax.dot_general(a, b, (((1,), (1,)), ((), ())), preferred_element_type=F32)


def tn(a, b):
    return lax.dot_general(a, b, (((0,), (0,)), ((), ())), preferred_element_type=F32)


def times(n, step):
    return pl.ds(pl.multiple_of(n, step), step)


def kernel(
    docs,
    q_hbm,
    k_hbm,
    v_hbm,
    og_hbm,
    w_hbm,
    lo_out,
    dq_out,
    dk_out,
    dv_out,
    wg_out,
    qkv,
    kvb,
    og_x,
    og_y,
    wo,
    mg,
    mixc,
    mx_x,
    mx_y,
    mx,
    probs,
    bias_l,
    bias_m,
    bias_f,
    sel,
    dkv,
    dqb,
    sb,
    rm,
    rfx,
    fs,
    rfz,
    far_sum,
    spread,
    outs,
    lob,
    t_x,
    t_y,
    r1_x,
    r1_y,
    s2_x,
    s2_y,
    r2_x,
    r2_y,
    s3_x,
    s3_y,
    wgr,
    send_sem,
    recv_sem,
    local_sem,
    last_send,
    last_recv,
):
    c, d = lax.axis_index("ctx"), lax.axis_index("dp")
    x, zl, j = lax.div(c, 4), lax.rem(lax.div(c, 2), 2), lax.rem(c, 2)
    zh, y = lax.div(d, 4), lax.rem(d, 4)
    z = zh * 2 + zl
    og_g, mx_g, t_g = (og_x, og_y), (mx_x, mx_y), (t_x, t_y)
    r1_g, s2_g, r2_g, s3_g = (r1_x, r1_y), (s2_x, s2_y), (r2_x, r2_y), (s3_x, s3_y)

    def at(x_=None, zl_=None, j_=None, zh_=None, y_=None):
        cx = (x if x_ is None else x_) * 4 + (zl if zl_ is None else zl_) * 2 + (j if j_ is None else j_)
        return (cx, (zh if zh_ is None else zh_) * 4 + (y if y_ is None else y_))

    def diagonal_peer(k):
        return at(x_=lax.rem(x + k, 4), y_=lax.rem(y + 4 - k, 4))

    def x_peer(k):
        return at(x_=lax.rem(x + k, 4))

    def y_peer(k):
        return at(y_=lax.rem(y + k, 4))

    def z_peer(k):
        other = lax.rem(z + k, 4)
        return at(zl_=lax.rem(other, 2), zh_=lax.div(other, 2))

    partner, neighbour = at(j_=1 - j), at(zl_=1 - zl)
    in_flight = []

    class Sent:
        def __init__(self, src, dst, device):
            n = sum(isinstance(copy, Sent) for copy in in_flight)
            in_flight.append(self)
            self.landed = False
            self.copy = pltpu.make_async_remote_copy(
                src_ref=src,
                dst_ref=dst,
                send_sem=send_sem.at[n],
                recv_sem=recv_sem.at[n],
                device_id=device,
                device_id_type=MESH,
            )
            self.copy.start()

        def wait_recv(self):
            if not self.landed:
                self.landed = True
                self.copy.wait_recv()

        def finish(self):
            self.wait_recv()
            self.copy.wait_send()

    class Local:
        def __init__(self, src, dst):
            n = sum(isinstance(copy, Local) for copy in in_flight)
            in_flight.append(self)
            self.done = False
            self.copy = pltpu.make_async_copy(src, dst, local_sem.at[n])
            self.copy.start()

        def wait(self):
            if not self.done:
                self.done = True
                self.copy.wait()

        finish = wait

    def drain():
        for copy in in_flight:
            copy.finish()

    own = times(j * 128, 128)
    theirs = times((1 - j) * 128, 128)

    def mine(b):
        return times(256 * (2 * b + j), 256)

    def not_mine(b):
        return times(256 * (2 * b + 1 - j), 256)

    def block(b):
        return pl.ds(256 * b, 256)

    in_kv = [
        Local(hbm.at[:, mine(b)], qkv.at[i, own, block(b)])
        for i, hbm in ((1, k_hbm), (2, v_hbm))
        for b in range(4)
    ]
    in_og = [
        Local(og_hbm.at[:, pl.ds(c0, nc)], og_g[g].at[a, own])
        for g, (a, (_, c0, nc)) in enumerate(zip((x, y), GATHERS))
    ]
    in_w = [Local(w_hbm.at[mine(b)], wo.at[mine(b)]) for b in range(4)]
    in_q = [Local(q_hbm.at[:, mine(b)], qkv.at[0, own, block(b)]) for b in range(4)]
    in_w2 = [Local(w_hbm.at[not_mine(b)], wo.at[not_mine(b)]) for b in range(4)]

    barrier = pltpu.get_barrier_semaphore()
    near = [partner] + [
        peer(k) for peer in (x_peer, y_peer, z_peer, diagonal_peer) for k in (1, 2, 3)
    ]
    for device in near:
        pl.semaphore_signal(barrier, inc=1, device_id=device, device_id_type=MESH)
    for n in range(8):
        a, b = 2 * j + n // 4, n % 4
        from_x = at(zl_=n // 4, j_=zl, zh_=j, y_=b)
        from_y = at(x_=a, zl_=b % 2, j_=zl, zh_=b // 2, y_=lax.rem(x + 4 - a, 4))
        for cc, dd in (from_x, from_y):

            @pl.when(jnp.logical_or(cc != c, dd != d))
            def _(cc=cc, dd=dd):
                pl.semaphore_signal(barrier, inc=1, device_id=(cc, dd), device_id_type=MESH)

    owner_x = x * 4 + j * 2 + zh
    owner_y = lax.rem(x + y, 4) * 4 + j * 2 + lax.div(x, 2)
    away = 16 - (owner_x == c).astype(jnp.int32) - (owner_y == c).astype(jnp.int32)
    pl.semaphore_wait(barrier, len(near) + away)

    swap_kv = [
        Sent(hbm.at[:, not_mine(b)], qkv.at[i, own, block(b)], partner)
        for i, hbm in ((1, k_hbm), (2, v_hbm))
        for b in range(4)
    ]
    def gather(g):
        a, peer = ((x, x_peer), (y, y_peer))[g]
        _, c0, nc = GATHERS[g]
        return [Sent(og_hbm.at[:, pl.ds(c0, nc)], og_g[g].at[a, own], peer(k)) for k in (1, 3)]

    def relay(g, copies):
        a, peer = ((x, x_peer), (y, y_peer))[g]
        passed = []
        for n, (k, copy) in enumerate(zip((1, 3), copies)):
            copy.wait_recv()
            ref = og_g[g].at[lax.rem(a + 4 - k, 4), pl.ds(pl.multiple_of(128 * j + 64 * n, 64), 64)]
            passed.append(Sent(ref, ref, peer(k)))
        return passed

    def to_partner(g, k):
        a = (x, y)[g]
        ref = og_g[g].at[lax.rem(a + k, 4), own]
        return Sent(ref, ref, partner)


    row = lax.broadcasted_iota(jnp.int32, (256, 256), 0)
    col = lax.broadcasted_iota(jnp.int32, (256, 256), 1)
    far_head = lax.shift_right_logical(row - 128, 4)
    mid_row = 4 * (row & 63) + 2 * j + (lax.shift_right_logical(row, 6) & 1)
    far_row = 16 * (row & 15) + 4 * lax.shift_right_logical(far_head, 1) + 2 * j + (far_head & 1)
    sel[...] = (col == jnp.where(row < 128, mid_row, far_row)).astype(F32).astype(BF)

    base = x * 512 + zl * 256
    here = lax.broadcasted_iota(jnp.int32, (256, 128), 0)
    key = lax.broadcasted_iota(jnp.int32, (256, 128), 1)
    pos = base + here
    start = jnp.zeros((256, 128), jnp.int32)
    end = jnp.int32(0)
    for n in range(8):
        end = end + docs[0, n]
        start = jnp.where(pos >= end, end, start)

    def shown(key_pos, extra):
        seen = jnp.logical_and(key_pos <= pos, key_pos >= start)
        if extra is not None:
            seen = jnp.logical_and(seen, extra)
        return jnp.where(seen, 0.0, HIDE).astype(F32)

    bias_l[...] = shown(base + (here & 128) + key, None)
    for e in range(2):
        r = 2 * j + e
        bias_m[e] = shown(x * 512 + 4 * key + r, (here & 3) == r)
    for hh in range(8):
        h = 4 * (hh // 2) + 2 * j + hh % 2
        bias_f[hh] = shown(16 * key + h, (here & 15) == h)

    far_own = pl.ds(pl.multiple_of(128 + 16 * (2 * x + zl), 16), 16)
    far_near = pl.ds(pl.multiple_of(128 + 16 * (2 * x + 1 - zl), 16), 16)
    mid_own = times(64 * zl, 64)
    for i in (0, 1):
        for copy in in_kv[4 * i : 4 * i + 4]:
            copy.wait()
        for copy in swap_kv[4 * i : 4 * i + 4]:
            copy.wait_recv()
        picked = nn(sel[...], qkv[1 + i]).astype(BF)
        for hh in range(8):
            hc = slice(HD * hh, HD * hh + HD)
            e = hh % 2
            kvb[i, mid_own, hc] = picked[64 * e : 64 * e + 64, hc]
            kvb[i, far_own, hc] = picked[128 + 16 * hh : 144 + 16 * hh, hc]
    far_z = Sent(kvb.at[:, far_own], kvb.at[:, far_own], neighbour)
    far_x = [Sent(kvb.at[:, far_own], kvb.at[:, far_own], x_peer(k)) for k in (1, 2, 3)]

    mid_sent = [Sent(kvb.at[:, mid_own], kvb.at[:, mid_own], neighbour)]
    swap_og = [
        Sent(og_hbm.at[:, pl.ds(c0, nc)], og_g[g].at[a, own], partner)
        for g, (a, (_, c0, nc)) in enumerate(zip((x, y), GATHERS))
    ]
    swap_q = [Sent(q_hbm.at[:, not_mine(b)], qkv.at[0, own, block(b)], partner) for b in range(4)]
    gather_y = gather(1)
    for copy in in_og:
        copy.wait()
    for copy in swap_og:
        copy.wait_recv()

    def mixed_grad_block(b):
        in_w[b].wait()
        part = nt(og_x[x], wo[mine(b), :HALF]) + nt(og_y[y], wo[mine(b), HALF:])
        mg[:, 256 * b : 256 * b + 256] = part.astype(BF)

    mixed_grad_block(0)
    far_z.wait_recv()
    far_fwd = [Sent(kvb.at[:, far_near], kvb.at[:, far_near], x_peer(k)) for k in (1, 2, 3)]
    gather_x = gather(0)
    for b in (1, 2, 3):
        mixed_grad_block(b)
    relay_y = relay(1, gather_y)
    forwarded = [to_partner(1, k) for k in (1, 3)]
    for copy in in_q:
        copy.wait()
    for copy in swap_q + mid_sent + far_x + far_fwd:
        copy.wait_recv()

    def halves(f, *operands):
        return jnp.concatenate([f(*(o[:128] for o in operands)), f(*(o[128:] for o in operands))], axis=0)

    def forward(hh, carry):
        hc = times(hh * HD, HD)
        q = qkv[0, :, hc]
        s_l = halves(nt, q, qkv[1, :, hc]) * (SCALE * LOG2E) + bias_l[...]
        s_b = nt(q, kvb[0, :, hc]) * (SCALE * LOG2E)
        s_m = s_b[:, :128] + bias_m[lax.rem(hh, 2)]
        s_f = s_b[:, 128:] + bias_f[hh]
        top = jnp.max(jnp.maximum(jnp.maximum(s_l, s_m), s_f), axis=1, keepdims=True)
        e_l, e_m, e_f = jnp.exp2(s_l - top), jnp.exp2(s_m - top), jnp.exp2(s_f - top)
        inv = 1.0 / jnp.sum(e_l + e_m + e_f, axis=1, keepdims=True)
        p_l = (e_l * inv).astype(BF)
        p_b = jnp.concatenate([(e_m * inv).astype(BF), (e_f * inv).astype(BF)], axis=1)
        probs[hh, :, :128] = p_l
        probs[hh, :, 128:] = p_b
        mixc[:, hc] = (halves(nn, p_l, qkv[2, :, hc]) + nn(p_b, kvb[1, :, hc])).astype(BF)
        return carry

    lax.fori_loop(0, 8, forward, 0, unroll=8)

    mix_sent = []
    for g, (a, peer, first) in enumerate(((x, x_peer, 0), (y, y_peer, x))):
        mx_g[g][a] = mixc[:, times(256 * lax.rem(first + a, 4), 256)]
        mix_sent.append(
            [
                Sent(mixc.at[:, times(256 * lax.rem(first + a + k, 4), 256)], mx_g[g].at[a], peer(k))
                for k in (1, 2, 3)
            ]
        )
    swap_mx = [
        Sent(mixc.at[theirs, block(b)], mx.at[:, mine(b)], partner) for b in range(4)
    ]
    for b in range(4):
        mx[:, mine(b)] = mixc[own, 256 * b : 256 * b + 256]

    relay_x = relay(0, gather_x)
    forwarded += [to_partner(0, k) for k in (1, 3)]

    def backward(hh, carry):
        hc = times(hh * HD, HD)
        q, gr = qkv[0, :, hc], mg[:, hc]
        delta = jnp.sum(gr.astype(F32) * mixc[:, hc].astype(F32), axis=1, keepdims=True)
        p_l, p_b = probs[hh, :, :128], probs[hh, :, 128:]
        ds_l = (p_l.astype(F32) * (halves(nt, gr, qkv[2, :, hc]) - delta)).astype(BF)
        ds_b = (p_b.astype(F32) * (nt(gr, kvb[1, :, hc]) - delta)).astype(BF)
        dq = halves(nn, ds_l, qkv[1, :, hc]) + nn(ds_b, kvb[0, :, hc])
        dqb[:, hc] = (dq * SCALE).astype(BF)
        dkv[0, :, hc] = halves(tn, ds_l, q)
        dkv[1, :, hc] = halves(tn, p_l, gr)
        sb[0, :, hc] = tn(ds_b, q).astype(BF)
        sb[1, :, hc] = tn(p_b, gr).astype(BF)
        return carry

    lax.fori_loop(0, 8, backward, 0, unroll=8)

    mid_back = Sent(sb.at[:, times(64 * (1 - zl), 64)], rm, neighbour)
    far_back = [
        Sent(sb.at[:, pl.ds(pl.multiple_of(128 + 32 * lax.rem(x + k, 4), 32), 32)], rfx.at[k - 1], x_peer(k))
        for k in (1, 2, 3)
    ]

    def give(buf, out):
        for b in range(4):
            Local(buf.at[own, block(b)], out.at[:, mine(b)])
            Sent(buf.at[theirs, block(b)], out.at[:, mine(b)], partner)

    for g, passed in ((1, relay_y), (0, relay_x)):
        for copy in passed:
            copy.wait_recv()
        forwarded.append(to_partner(g, 2))
    give(dqb, dq_out)

    for copy in forwarded:
        copy.wait_recv()
    around = (z, z_peer), (x, diagonal_peer)
    turned = []
    for g in range(2):
        for copy in mix_sent[g]:
            copy.wait_recv()
        turned.append(mx_g[g][...].reshape(HALF, 256).T)
    sent_1 = []
    for g, n in UNITS:
        for c0 in range(PART * n, PART * n + PART, 256):
            cols = slice(c0, c0 + 256)
            t_g[g][:, cols] = nn(turned[g], og_g[g][:, :, cols].reshape(HALF, 256)).astype(BF)
        cols = pl.ds(PART * n, PART)
        a, peer = around[g]
        sent_1.append(
            [
                Sent(t_g[g].at[times(64 * lax.rem(a + k, 4), 64), cols], r1_g[g].at[k - 1, :, cols], peer(k))
                for k in (1, 2, 3)
            ]
        )

    for copy in in_w2:
        copy.wait()
    for copy in swap_mx:
        copy.wait_recv()

    def out_block(n, carry):
        cols = times(n * 512, 512)
        lob[:, cols] = nn(mx[...], wo[:, cols]).astype(BF)
        return carry

    lax.fori_loop(0, 4, out_block, 0)
    Local(lob, lo_out)

    for copy in far_back:
        copy.wait_recv()
    far_sum[...] = sb[:, pl.ds(pl.multiple_of(128 + 32 * x, 32), 32)].astype(F32)
    for k in range(3):
        far_sum[...] += rfx[k].astype(F32)
    fs[...] = far_sum[:, times(16 * (1 - zl), 16)].astype(BF)
    far_last = Sent(fs, rfz, neighbour)

    around_2 = (y, y_peer), (z, z_peer)
    sent_2 = []
    for (g, n), copies in zip(UNITS, sent_1):
        for copy in copies:
            copy.wait_recv()
        cols = slice(PART * n, PART * n + PART)
        total = t_g[g][times(64 * around[g][0], 64), cols].astype(F32)
        for k in range(3):
            total = total + r1_g[g][k, :, cols].astype(F32)
        s2_g[g][:, cols] = total.astype(BF)
        cols = pl.ds(PART * n, PART)
        a, peer = around_2[g]
        sent_2.append(
            [
                Sent(s2_g[g].at[times(16 * lax.rem(a + k, 4), 16), cols], r2_g[g].at[k - 1, :, cols], peer(k))
                for k in (1, 2, 3)
            ]
        )

    piece = lax.rem(4 * zl + y, 8), lax.rem(4 * lax.rem(x, 2) + z, 8)
    owners = owner_x, owner_y
    for m, ((g, n), copies) in enumerate(zip(UNITS, sent_2)):
        for copy in copies:
            copy.wait_recv()
        cols = slice(PART * n, PART * n + PART)
        total = s2_g[g][times(16 * around_2[g][0], 16), cols].astype(F32)
        for k in range(3):
            total = total + r2_g[g][k, :, cols].astype(F32)
        s3_g[g][:, cols] = total.astype(BF)
        src = s3_g[g].at[:, pl.ds(PART * n, PART)]
        dst = wgr.at[times(16 * piece[g], 16), pl.ds(GATHERS[g][1] + PART * n, PART)]
        for dp in range(8):
            stays = jnp.logical_and(owners[g] == c, d == dp)

            @pl.when(stays)
            def _(m=m, g=g, src=src, dst=dst):
                pltpu.make_async_copy(src, dst, last_recv.at[8 * m + piece[g]]).start()

            @pl.when(jnp.logical_not(stays))
            def _(m=m, g=g, dp=dp, src=src, dst=dst):
                pltpu.make_async_remote_copy(
                    src_ref=src,
                    dst_ref=dst,
                    send_sem=last_send.at[8 * m + dp],
                    recv_sem=last_recv.at[8 * m + piece[g]],
                    device_id=(owners[g], jnp.int32(dp)),
                    device_id_type=MESH,
                ).start()

    mid_back.wait_recv()
    far_last.wait_recv()
    far_mine = times(16 * zl, 16)
    for i, out in ((0, dk_out), (1, dv_out)):
        spread[...] = jnp.zeros_like(spread)
        for hh in range(8):
            hc = slice(HD * hh, HD * hh + HD)
            e = hh % 2
            spread[64 * e : 64 * e + 64, hc] = (
                sb[i, mid_own, hc].astype(F32) + rm[i, :, hc].astype(F32)
            ).astype(BF)
            spread[128 + 16 * hh : 144 + 16 * hh, hc] = (
                far_sum[i, far_mine, hc] + rfz[i, :, hc].astype(F32)
            ).astype(BF)
        total = dkv[i] + tn(sel[...], spread[...])
        outs[i] = (total * SCALE if i == 0 else total).astype(BF)
        give(outs.at[i], out)

    for m, (g, n) in enumerate(UNITS):
        src = s3_g[g].at[:, pl.ds(PART * n, PART)]
        for k in range(8):
            ref = wgr.at[pl.ds(16 * k, 16), pl.ds(GATHERS[g][1] + PART * n, PART)]
            pltpu.make_async_copy(src, ref, last_recv.at[8 * m + k]).wait()
    Local(wgr, wg_out)

    for m, (g, n) in enumerate(UNITS):
        src = s3_g[g].at[:, pl.ds(PART * n, PART)]
        for dp in range(8):

            @pl.when(jnp.logical_not(jnp.logical_and(owners[g] == c, d == dp)))
            def _(m=m, dp=dp, src=src):
                pltpu.make_async_copy(src, src, last_send.at[8 * m + dp]).wait()

    drain()


def place(lo, dq, dk, dv, wg, lo_out, dq_out, dk_out, dv_out, wg_out, held, wg32, sems):
    pairs = ((wg, None), (lo, lo_out), (dq, dq_out), (dk, dk_out), (dv, dv_out))
    taken = [pltpu.make_async_copy(src, held.at[n], sems.at[n]) for n, (src, _) in enumerate(pairs)]
    for copy in taken:
        copy.start()
    given = []
    for n, (_, dst) in enumerate(pairs):
        taken[n].wait()
        if dst is None:
            wg32[...] = held[n].astype(F32)
        given.append(
            pltpu.make_async_copy(wg32 if dst is None else held.at[n], wg_out if dst is None else dst, sems.at[5 + n])
        )
        given[n].start()
    for copy in given:
        copy.wait()


def shards(queries, key_states, value_states, out_grad, w_out, doc_lengths):
    rows = queries.shape[1]
    hbm = pl.BlockSpec(memory_space=pl.ANY)
    out16 = jax.ShapeDtypeStruct((rows, WIDTH), BF)
    vm = pltpu.VMEM
    outs = pl.pallas_call(
        kernel,
        out_shape=[out16] * 5,
        in_specs=[pl.BlockSpec(memory_space=pltpu.SMEM)] + [hbm] * 5,
        out_specs=[hbm] * 5,
        scratch_shapes=[
            vm((3, 256, HALF), BF),
            vm((2, 256, HALF), BF),
            vm((4, 256, HALF), BF),
            vm((4, 256, HALF), BF),
            vm((WIDTH, WIDTH), BF),
            vm((256, HALF), BF),
            vm((256, HALF), BF),
            vm((4, 256, 256), BF),
            vm((4, 256, 256), BF),
            vm((128, WIDTH), BF),
            vm((8, 256, 384), BF),
            vm((256, 128), F32),
            vm((2, 256, 128), F32),
            vm((8, 256, 128), F32),
            vm((256, 256), BF),
            vm((2, 256, HALF), F32),
            vm((256, HALF), BF),
            vm((2, 256, HALF), BF),
            vm((2, 64, HALF), BF),
            vm((3, 2, 32, HALF), BF),
            vm((2, 16, HALF), BF),
            vm((2, 16, HALF), BF),
            vm((2, 32, HALF), F32),
            vm((256, HALF), BF),
            vm((2, 256, HALF), BF),
            vm((128, WIDTH), BF),
            vm((256, HALF), BF),
            vm((256, HALF), BF),
            vm((3, 64, HALF), BF),
            vm((3, 64, HALF), BF),
            vm((64, HALF), BF),
            vm((64, HALF), BF),
            vm((3, 16, HALF), BF),
            vm((3, 16, HALF), BF),
            vm((16, HALF), BF),
            vm((16, HALF), BF),
            vm((128, WIDTH), BF),
            pltpu.SemaphoreType.DMA((96,)),
            pltpu.SemaphoreType.DMA((96,)),
            pltpu.SemaphoreType.DMA((40,)),
            pltpu.SemaphoreType.DMA((32,)),
            pltpu.SemaphoreType.DMA((32,)),
        ],
        compiler_params=pltpu.CompilerParams(
            collective_id=0, has_side_effects=True, vmem_limit_bytes=56 << 20
        ),
        name="dilated_attention",
    )(doc_lengths, queries[0], key_states[0], value_states[0], out_grad[0], w_out)
    outs = pl.pallas_call(
        place,
        out_shape=[out16] * 4 + [jax.ShapeDtypeStruct((rows, WIDTH), F32)],
        in_specs=[hbm] * 5,
        out_specs=[hbm] * 5,
        scratch_shapes=[vm((5, rows, WIDTH), BF), vm((rows, WIDTH), F32), pltpu.SemaphoreType.DMA((10,))],
        name="place_results",
    )(*outs)
    return tuple(o[None] for o in outs[:4]) + (outs[4],)


def solution(mesh):
    rows = P("dp", "ctx", None)
    return jax.shard_map(
        shards,
        mesh=mesh,
        in_specs=(rows, rows, rows, rows, P(), P("dp", None)),
        out_specs=(rows, rows, rows, rows, P("ctx", None)),
        check_vma=False,
    )
```
